32 devices in a mesh: rep: 8 (over z, core), shard: 4 (over y, x).
Axes of the slice: x: 2, y: 2, z: 4, core: 2. Of those that a mesh axis runs over, the one named last changes fastest.
Arguments:
- tokens: bfloat16 [4096, 1024], P(('rep', 'shard')), may hold values from -6 to 6
- cotangent: bfloat16 [4096, 1024], P(('rep', 'shard')), may hold values from -6 to 6
- seq_len: int32 [128], P(('rep', 'shard')), may hold values from 0 to 128, as said below
- in_proj: float32 [1024, 4096], P('shard'), may hold values from -0.1875 to 0.1875
- in_proj_first: float32 [1024, 4096], P('shard', 'rep'), may hold values from -0.0390625 to 0.0390625
- in_proj_second: float32 [1024, 4096], P('shard', 'rep'), may hold values from 1.2207031e-05 to 0.00021972656
- dt_proj: float32 [1024, 24], P('shard'), may hold values from -0.1875 to 0.1875
- dt_proj_first: float32 [1024, 24], P('shard'), may hold values from -0.0390625 to 0.0390625
- dt_proj_second: float32 [1024, 24], P('shard'), may hold values from 1.2207031e-05 to 0.00021972656
- out_proj: float32 [2048, 1024], P('shard'), may hold values from -0.125 to 0.125
- out_proj_first: float32 [2048, 1024], P('shard', 'rep'), may hold values from -0.0390625 to 0.0390625
- out_proj_second: float32 [2048, 1024], P('shard', 'rep'), may hold values from 1.2207031e-05 to 0.00021972656
- gate_up: float32 [1024, 4096], P('shard'), may hold values from -0.1875 to 0.1875
- gate_up_first: float32 [1024, 4096], P('shard', 'rep'), may hold values from -0.0390625 to 0.0390625
- gate_up_second: float32 [1024, 4096], P('shard', 'rep'), may hold values from 1.2207031e-05 to 0.00021972656
- down_proj: float32 [2048, 1024], P('shard'), may hold values from -0.125 to 0.125
- down_proj_first: float32 [2048, 1024], P('shard', 'rep'), may hold values from -0.0390625 to 0.0390625
- down_proj_second: float32 [2048, 1024], P('shard', 'rep'), may hold values from 1.2207031e-05 to 0.00021972656
- norm_gains: float32 [3584], P('shard'), may hold values from 0.5 to 1.5
- gains_first: float32 [3584], P('shard'), may hold values from -0.0390625 to 0.0390625
- gains_second: float32 [3584], P('shard'), may hold values from 1.2207031e-05 to 0.00021972656
- conv_taps: float32 [5, 1792], P(None, 'shard'), may hold values from -3 to 3
- conv_first: float32 [5, 1792], P(None, 'shard'), may hold values from -0.0390625 to 0.0390625
- conv_second: float32 [5, 1792], P(None, 'shard'), may hold values from 1.2207031e-05 to 0.00021972656
- ssm_params: float32 [3, 24], replicated, may hold values from -4.5 to 3, as said below
- ssm_first: float32 [3, 24], replicated, may hold values from -0.3125 to 0.3125
- ssm_second: float32 [3, 24], replicated, may hold values from 0.00012207031 to 0.0009765625
Outputs:
- output: bfloat16 [4096, 1024], P(('rep', 'shard'))
- token_grad: bfloat16 [4096, 1024], P(('rep', 'shard'))
- in_proj_first_new: float32 [1024, 4096], P('shard', 'rep')
- in_proj_second_new: float32 [1024, 4096], P('shard', 'rep')
- in_proj_new: float32 [1024, 4096], P('shard')
- dt_proj_first_new: float32 [1024, 24], P('shard')
- dt_proj_second_new: float32 [1024, 24], P('shard')
- dt_proj_new: float32 [1024, 24], P('shard')
- out_proj_first_new: float32 [2048, 1024], P('shard', 'rep')
- out_proj_second_new: float32 [2048, 1024], P('shard', 'rep')
- out_proj_new: float32 [2048, 1024], P('shard')
- gate_up_first_new: float32 [1024, 4096], P('shard', 'rep')
- gate_up_second_new: float32 [1024, 4096], P('shard', 'rep')
- gate_up_new: float32 [1024, 4096], P('shard')
- down_proj_first_new: float32 [2048, 1024], P('shard', 'rep')
- down_proj_second_new: float32 [2048, 1024], P('shard', 'rep')
- down_proj_new: float32 [2048, 1024], P('shard')
- gains_first_new: float32 [3584], P('shard')
- gains_second_new: float32 [3584], P('shard')
- gains_new: float32 [3584], P('shard')
- conv_first_new: float32 [5, 1792], P(None, 'shard')
- conv_second_new: float32 [5, 1792], P(None, 'shard')
- conv_new: float32 [5, 1792], P(None, 'shard')
- ssm_first_new: float32 [3, 24], replicated
- ssm_second_new: float32 [3, 24], replicated
- ssm_new: float32 [3, 24], replicated
The draws below stay inside these ranges and needn't reach their ends.
Inputs may be any that keep to these rules, and one draw needn't show every extreme that they name: `seq_len`: each device's 4 lengths sum to at most 128; the last device holds one sequence of exactly 128 tokens and its other slots are empty. `ssm_params`: row 0 holds log decay rates, row 1 step offsets, row 2 skip gains.
All inputs are finite; a program needn't handle non-finite values.
Results may differ from the reference program's by a relative error of at most 0.011.
The reference program's roundings to bfloat16 on the way count: a program that leaves them out, or rounds other values in their place, can miss the bound.
Values may be sent and summed in bfloat16 or wider, within the bound.
A program may use at most 128 MiB of HBM per device.

```python
import math
import jax
import jax.numpy as jnp
from jax import lax

D = 1024
MIXER_HEADS = 24
MIXER_HEAD_SIZE = 64
NS = 128
QUERY_HEADS = 8
KEY_VALUE_HEADS = 2
HEAD_SIZE = 64
FF = 2048
KCONV = 4
TOK_DEV = 128
SLOTS = 4
STEP = 10
MIXER_WIDTH = 1536
CONV = 1792
NIN = 4096
NOUT = 2048
NGAIN = 3584
REPLICAS = 8
GROUP = 4
TOKENS = 4096


def draw_seq_len(key, part):
    key = jax.random.fold_in(key, 11)
    device_total = REPLICAS * GROUP
    device_ids = jnp.arange(device_total, dtype=jnp.int32)
    rep_share = 50 + 50 * (device_ids // GROUP) // max(REPLICAS - 1, 1)
    shard_share = 50 + 50 * (device_ids % GROUP) // max(GROUP - 1, 1)
    jitter_key, split_key = jax.random.split(key)
    jitter = jax.random.randint(jitter_key, (device_total,), 85, 101, dtype=jnp.int32)
    jitter = jnp.where(device_ids == device_total - 1, 100, jitter)
    live_rows = TOK_DEV * rep_share * shard_share // 10000 * jitter // 100
    cuts = jax.random.randint(split_key, (device_total, SLOTS - 1), 0, 1 << 20, dtype=jnp.int32) % (live_rows[:, None] + 1)
    cuts = jnp.where((device_ids == device_total - 1)[:, None], 0, cuts)
    cuts = jnp.sort(cuts, axis=1)
    bounds = jnp.concatenate([jnp.zeros((device_total, 1), jnp.int32), cuts, live_rows[:, None]], axis=1)
    return (bounds[:, 1:] - bounds[:, :-1]).reshape(-1).astype(jnp.int32)


def draw_ssm_params(key, part):
    key = jax.random.fold_in(key, 12)
    spread = jax.random.uniform(key, (3, MIXER_HEADS), jnp.float32)
    log_decay = jnp.log(1.0 + 15.0 * spread[0])
    dt_offset = -4.5 + 3.0 * spread[1]
    skip_gain = 0.5 + spread[2]
    return jnp.stack([log_decay, dt_offset, skip_gain])


def block_levels(rng, shape, cuts, low, top_value):
    level = 1.0
    for axis_at, parts in cuts:
        heights = jax.random.uniform(jax.random.fold_in(jax.random.fold_in(rng, 6), axis_at), (parts,), jnp.float32, low / len(cuts), top_value / len(cuts))
        level = level * jnp.repeat(jnp.exp(heights), shape[axis_at] // parts).reshape((-1,) + (1,) * (len(shape) - 1 - axis_at))
    return level


def centred(key, shape, width, most, cuts=(), held_as=jnp.bfloat16):
    entries = jax.random.normal(key, shape, jnp.float32) * width
    if len(cuts) > 0:
        entries = block_levels(key, shape, cuts, -0.22, 0.18) * entries
    return jnp.clip(entries, min=-most, max=most).astype(held_as)


def setup_inputs(seed: int = 0) -> dict:
    splits = jax.random.split(jax.random.key(seed), 28)
    tokens = centred(splits[0], (TOKENS, D), 1.0, 6.0, ((0, 32),))
    cotangent = centred(splits[1], (TOKENS, D), 1.0, 6.0, ((0, 32),))
    seq_len = draw_seq_len(jax.random.fold_in(splits[27], 71), 0)
    in_proj = centred(splits[3], (D, NIN), D ** -0.5, 0.1875, ((0, 4),), jnp.float32)
    in_proj_first = centred(splits[4], (D, NIN), (0.16 * TOKENS ** -0.5), 0.0390625, ((0, 4), (1, 8)), jnp.float32)
    in_proj_second = jnp.clip(jnp.exp(math.log(0.00021972656) - 2.8903717 * jax.random.uniform(splits[5], (D, NIN), jnp.float32) ** block_levels(splits[5], (D, NIN), ((0, 4), (1, 8)), -0.2, 0.2)), 1.220703143189894e-05, 0.00021972656)
    dt_proj = centred(splits[6], (D, MIXER_HEADS), D ** -0.5, 0.1875, ((0, 4),), jnp.float32)
    dt_proj_first = centred(splits[7], (D, MIXER_HEADS), (0.16 * TOKENS ** -0.5), 0.0390625, ((0, 4),), jnp.float32)
    dt_proj_second = jnp.clip(jnp.exp(math.log(0.00021972656) - 2.8903717 * jax.random.uniform(splits[8], (D, MIXER_HEADS), jnp.float32) ** block_levels(splits[8], (D, MIXER_HEADS), ((0, 4),), -0.2, 0.2)), 1.220703143189894e-05, 0.00021972656)
    out_proj = centred(splits[9], (NOUT, D), NOUT ** -0.5, 0.125, ((0, 4),), jnp.float32)
    out_proj_first = centred(splits[10], (NOUT, D), (0.16 * TOKENS ** -0.5), 0.0390625, ((0, 4), (1, 8)), jnp.float32)
    out_proj_second = jnp.clip(jnp.exp(math.log(0.00021972656) - 2.8903717 * jax.random.uniform(splits[11], (NOUT, D), jnp.float32) ** block_levels(splits[11], (NOUT, D), ((0, 4), (1, 8)), -0.2, 0.2)), 1.220703143189894e-05, 0.00021972656)
    gate_up = centred(splits[12], (D, 2 * FF), D ** -0.5, 0.1875, ((0, 4),), jnp.float32)
    gate_up_first = centred(splits[13], (D, 2 * FF), (0.16 * TOKENS ** -0.5), 0.0390625, ((0, 4), (1, 8)), jnp.float32)
    gate_up_second = jnp.clip(jnp.exp(math.log(0.00021972656) - 2.8903717 * jax.random.uniform(splits[14], (D, 2 * FF), jnp.float32) ** block_levels(splits[14], (D, 2 * FF), ((0, 4), (1, 8)), -0.2, 0.2)), 1.220703143189894e-05, 0.00021972656)
    down_proj = centred(splits[15], (FF, D), FF ** -0.5, 0.125, ((0, 4),), jnp.float32)
    down_proj_first = centred(splits[16], (FF, D), (0.16 * TOKENS ** -0.5), 0.0390625, ((0, 4), (1, 8)), jnp.float32)
    down_proj_second = jnp.clip(jnp.exp(math.log(0.00021972656) - 2.8903717 * jax.random.uniform(splits[17], (FF, D), jnp.float32) ** block_levels(splits[17], (FF, D), ((0, 4), (1, 8)), -0.2, 0.2)), 1.220703143189894e-05, 0.00021972656)
    norm_gains = jnp.clip(1.0 + 0.1 * jax.random.normal(splits[18], (NGAIN,), jnp.float32), 0.5, 1.5)
    gains_first = centred(splits[19], (NGAIN,), (0.16 * TOKENS ** -0.5), 0.0390625, ((0, 4),), jnp.float32)
    gains_second = jnp.clip(jnp.exp(math.log(0.00021972656) - 2.8903717 * jax.random.uniform(splits[20], (NGAIN,), jnp.float32) ** block_levels(splits[20], (NGAIN,), ((0, 4),), -0.2, 0.2)), 1.220703143189894e-05, 0.00021972656)
    conv_taps = centred(splits[21], (KCONV + 1, CONV), KCONV ** -0.5, 3.0, ((1, 4),), jnp.float32)
    conv_first = centred(splits[22], (KCONV + 1, CONV), (0.16 * TOKENS ** -0.5), 0.0390625, ((1, 4),), jnp.float32)
    conv_second = jnp.clip(jnp.exp(math.log(0.00021972656) - 2.8903717 * jax.random.uniform(splits[23], (KCONV + 1, CONV), jnp.float32) ** block_levels(splits[23], (KCONV + 1, CONV), ((1, 4),), -0.2, 0.2)), 1.220703143189894e-05, 0.00021972656)
    ssm_params = draw_ssm_params(jax.random.fold_in(splits[27], 71), 0)
    ssm_first = centred(splits[25], (3, MIXER_HEADS), (1.3 * TOKENS ** -0.5), 0.3125, (), jnp.float32)
    ssm_second = jnp.clip(jnp.exp(jax.random.uniform(splits[26], (3, MIXER_HEADS), jnp.float32, math.log(0.00012207031), math.log(0.0009765625))), 0.00012207031, 0.0009765625)
    return dict(tokens=tokens, cotangent=cotangent, seq_len=seq_len, in_proj=in_proj, in_proj_first=in_proj_first, in_proj_second=in_proj_second, dt_proj=dt_proj, dt_proj_first=dt_proj_first, dt_proj_second=dt_proj_second, out_proj=out_proj, out_proj_first=out_proj_first, out_proj_second=out_proj_second, gate_up=gate_up, gate_up_first=gate_up_first, gate_up_second=gate_up_second, down_proj=down_proj, down_proj_first=down_proj_first, down_proj_second=down_proj_second, norm_gains=norm_gains, gains_first=gains_first, gains_second=gains_second, conv_taps=conv_taps, conv_first=conv_first, conv_second=conv_second, ssm_params=ssm_params, ssm_first=ssm_first, ssm_second=ssm_second)


@jax.custom_vjp
def reduced_precision(v):
    return lax.optimization_barrier(v.astype(jnp.bfloat16)).astype(jnp.float32)

@jax.custom_vjp
def low_back(v):
    return v

def low_keep(v):
    return (reduced_precision(v), None)

def low_pass(kept, grad):
    return (grad,)

def back_keep(v):
    return (v, None)

def back_low(kept, grad):
    return (reduced_precision(grad),)
reduced_precision.defvjp(low_keep, low_pass)
low_back.defvjp(back_keep, back_low)
precise = lax.Precision.HIGHEST
EPSILON_NORM = 1e-05
ROPE_BASE = 10000.0
NEG_BIG = -1e+30
ATT_MULT = 8.0
BETA_ONE = 0.9
BETA_TWO = 0.95
ADAM_EPS = 1e-08

def rms_scale(values, gain):
    return values * lax.rsqrt(lax.optimization_barrier(jnp.mean(values * values, axis=-1, keepdims=True)) + EPSILON_NORM) * gain

def layout(lengths, count_of_rows):
    lengths = lengths.astype(jnp.int32)
    seq_ends = jnp.cumsum(lengths).astype(jnp.int32)
    starts = (seq_ends - lengths).astype(jnp.int32)
    row_ids = jnp.arange(count_of_rows, dtype=jnp.int32)
    document = lax.optimization_barrier(jnp.sum((row_ids[:, None] >= seq_ends[None, :]).astype(jnp.int32), axis=1))
    row_alive = row_ids < seq_ends[-1]
    slot_ids = jnp.arange(lengths.shape[0], dtype=jnp.int32)
    first_row = lax.optimization_barrier(jnp.sum(jnp.where(document[:, None] == slot_ids[None, :], starts[None, :], 0), axis=1)).astype(jnp.int32)
    token_position = jnp.where(row_alive, row_ids - first_row, 0).astype(jnp.int32)
    same_doc = (document[:, None] == document[None, :]) & row_alive[None, :] & (row_ids[None, :] <= row_ids[:, None])
    pair_mask = same_doc | (row_ids[:, None] == row_ids[None, :])
    return (row_alive, token_position, pair_mask)

def apply_rotary(head_rows, token_position):
    half_width = head_rows.shape[-1] // 2
    frequency = ROPE_BASE ** (-jnp.arange(half_width, dtype=jnp.float32) / half_width)
    angles = token_position.astype(jnp.float32)[:, None] * frequency[None, :]
    cosine = jnp.cos(angles)[:, None, :]
    sine_part = jnp.sin(angles)[:, None, :]
    front = head_rows[..., :half_width]
    latter = head_rows[..., half_width:]
    return jnp.concatenate([front * cosine - latter * sine_part, latter * cosine + front * sine_part], axis=-1)

def rotary_pair(query_key_pair, token_position):
    count_of_rows = query_key_pair.shape[0]
    head_rows = query_key_pair.reshape(count_of_rows, QUERY_HEADS + KEY_VALUE_HEADS, HEAD_SIZE)
    return apply_rotary(head_rows, token_position).reshape(count_of_rows, (QUERY_HEADS + KEY_VALUE_HEADS) * HEAD_SIZE)

def swiglu(gate_vals):
    return jax.nn.silu(gate_vals[:, :FF]) * gate_vals[:, FF:]

def mixer_core(zxbc, conv_weight, ssm_weight, gain_mix, pair_mask, token_position):
    count_of_rows = zxbc.shape[0]
    gate_z = zxbc[:, :MIXER_WIDTH]
    conv_in = zxbc[:, MIXER_WIDTH:MIXER_WIDTH + CONV]
    dt_raw = zxbc[:, MIXER_WIDTH + CONV:MIXER_WIDTH + CONV + MIXER_HEADS]
    conv_sum = jnp.broadcast_to(conv_weight[KCONV][None, :], conv_in.shape)
    for tap_index in range(KCONV):
        lag_rows = KCONV - 1 - tap_index
        if lag_rows == 0:
            shifted = conv_in
        else:
            shifted = jnp.concatenate([jnp.zeros((lag_rows, CONV), conv_in.dtype), conv_in[:count_of_rows - lag_rows]], axis=0)
            shifted = jnp.where((token_position >= lag_rows)[:, None], shifted, 0.0)
        conv_sum = conv_sum + conv_weight[tap_index][None, :] * shifted
    convolved_output = jax.nn.silu(conv_sum)
    input_heads = convolved_output[:, :MIXER_WIDTH].reshape(count_of_rows, MIXER_HEADS, MIXER_HEAD_SIZE)
    b_rows = convolved_output[:, MIXER_WIDTH:MIXER_WIDTH + NS]
    c_rows = convolved_output[:, MIXER_WIDTH + NS:]
    dt_step = jax.nn.softplus(dt_raw + ssm_weight[1][None, :])
    decay_rate = -jnp.exp(ssm_weight[0])
    decay_cum = jnp.cumsum(dt_step * decay_rate[None, :], axis=0).T
    decay_gaps = decay_cum[:, :, None] - decay_cum[:, None, :]
    weights = jnp.exp(jnp.where(pair_mask[None], decay_gaps, NEG_BIG))
    inner_prod = jnp.dot(c_rows, b_rows.T, precision=precise)
    kernel = weights * inner_prod[None] * dt_step.T[:, None, :]
    mixed_out = jnp.einsum('hts,shd->thd', kernel, input_heads, precision=precise)
    mixed_out = mixed_out + ssm_weight[2][None, :, None] * input_heads
    gated_out = mixed_out.reshape(count_of_rows, MIXER_WIDTH) * jax.nn.silu(gate_z)
    return rms_scale(gated_out, gain_mix)

def attention(query_key_value_slice, pair_mask, token_position):
    count_of_rows = query_key_value_slice.shape[0]
    rotary_output = reduced_precision(rotary_pair(query_key_value_slice[:, :(QUERY_HEADS + KEY_VALUE_HEADS) * HEAD_SIZE], token_position))
    query_rows = rotary_output[:, :QUERY_HEADS * HEAD_SIZE].reshape(count_of_rows, KEY_VALUE_HEADS, QUERY_HEADS // KEY_VALUE_HEADS, HEAD_SIZE)
    key_reduced = rotary_output[:, QUERY_HEADS * HEAD_SIZE:].reshape(count_of_rows, KEY_VALUE_HEADS, HEAD_SIZE)
    value_reduced = reduced_precision(query_key_value_slice[:, (QUERY_HEADS + KEY_VALUE_HEADS) * HEAD_SIZE:]).reshape(count_of_rows, KEY_VALUE_HEADS, HEAD_SIZE)
    scores = low_back(jnp.einsum('tkgd,skd->kgts', query_rows, key_reduced, precision=precise) * HEAD_SIZE ** (-0.5))
    scores = jnp.where(pair_mask[None, None], scores, NEG_BIG)
    probs = reduced_precision(jax.nn.softmax(scores, axis=-1))
    attended = jnp.einsum('kgts,skd->tkgd', probs, value_reduced, precision=precise)
    return reduced_precision(low_back(attended.reshape(count_of_rows, QUERY_HEADS * HEAD_SIZE)))

def block_forward(rounded, block_tokens, block_lengths):
    in_weight, dt_weight, out_weight, gate_up_weight, down_weight, gain_weight, conv_weight, ssm_weight = rounded
    row_alive, token_position, pair_mask = layout(block_lengths, block_tokens.shape[0])
    normed = reduced_precision(rms_scale(block_tokens, gain_weight[:D]))
    joined = jnp.concatenate([in_weight[:, :MIXER_WIDTH + CONV], dt_weight, in_weight[:, MIXER_WIDTH + CONV:]], axis=1)
    projected_input = low_back(jnp.dot(normed, joined, precision=precise))
    split_boundary = MIXER_WIDTH + CONV + MIXER_HEADS
    mixer_low = reduced_precision(mixer_core(projected_input[:, :split_boundary], conv_weight, ssm_weight, gain_weight[2 * D:], pair_mask, token_position))
    attended = attention(projected_input[:, split_boundary:], pair_mask, token_position)
    branch_in = jnp.concatenate([mixer_low, ATT_MULT * attended], axis=1)
    branch = low_back(jnp.dot(branch_in, out_weight, precision=precise))
    hidden = block_tokens + branch
    normed_two = reduced_precision(rms_scale(hidden, gain_weight[D:2 * D]))
    gate_vals = low_back(jnp.dot(normed_two, gate_up_weight, precision=precise))
    act_low = reduced_precision(swiglu(gate_vals))
    return hidden + low_back(jnp.dot(act_low, down_weight, precision=precise))

def adam_update(param, first, second, grad, rate, decay):
    new_first = BETA_ONE * first + (1.0 - BETA_ONE) * grad
    new_second = BETA_TWO * second + (1.0 - BETA_TWO) * grad * grad
    first_hat = new_first / (1.0 - BETA_ONE ** STEP)
    second_hat = new_second / (1.0 - BETA_TWO ** STEP)
    new_param = param - rate * (first_hat / (jnp.sqrt(second_hat) + ADAM_EPS) + decay * param)
    return (new_first, new_second, new_param)

def reference(tokens, cotangent, seq_len, in_proj, in_proj_first, in_proj_second, dt_proj, dt_proj_first, dt_proj_second, out_proj, out_proj_first, out_proj_second, gate_up, gate_up_first, gate_up_second, down_proj, down_proj_first, down_proj_second, norm_gains, gains_first, gains_second, conv_taps, conv_first, conv_second, ssm_params, ssm_first, ssm_second):
    masters = (in_proj, dt_proj, out_proj, gate_up, down_proj, norm_gains, conv_taps, ssm_params)
    lengths = seq_len.reshape(-1, SLOTS)
    inputs = tokens.astype(jnp.float32)

    def whole(params, token_values):
        rounded = tuple((reduced_precision(param) for param in params[:7])) + (params[7],)
        run_block = jax.checkpoint(lambda block_tokens, block_lengths: block_forward(rounded, block_tokens, block_lengths))
        blocks = lax.map(lambda block_pair: run_block(block_pair[0], block_pair[1]), (token_values.reshape(-1, TOK_DEV, D), lengths))
        return blocks.reshape(-1, D)
    output, pullback = jax.vjp(whole, masters, inputs)
    row_alive = (jnp.arange(TOK_DEV, dtype=jnp.int32)[None, :] < lax.optimization_barrier(jnp.sum(lengths, axis=1))[:, None]).reshape(-1)
    upstream = cotangent.astype(jnp.float32) * row_alive[:, None].astype(jnp.float32)
    grads, token_grad = pullback(upstream)
    token_count = jnp.sum(seq_len).astype(jnp.float32)
    grad_in, grad_dt, grad_out, grad_gu, grad_down, grad_gains, grad_conv, grad_ssm = [grad / token_count for grad in grads]
    in_first_new, in_second_new, in_new = adam_update(in_proj, in_proj_first, in_proj_second, grad_in, 0.7 * D ** (-0.5), 0.1)
    dt_first_new, dt_second_new, dt_new = adam_update(dt_proj, dt_proj_first, dt_proj_second, grad_dt, 0.7 * D ** (-0.5), 0.1)
    out_first_new, out_second_new, out_new = adam_update(out_proj, out_proj_first, out_proj_second, grad_out, 0.7 * NOUT ** (-0.5), 0.1)
    gu_first_new, gu_second_new, gu_new = adam_update(gate_up, gate_up_first, gate_up_second, grad_gu, 0.7 * D ** (-0.5), 0.1)
    down_first_new, down_second_new, down_new = adam_update(down_proj, down_proj_first, down_proj_second, grad_down, 0.7 * FF ** (-0.5), 0.1)
    gain_first_new, gain_second_new, gain_new = adam_update(norm_gains, gains_first, gains_second, grad_gains, 0.3, 0.0)
    conv_first_new, conv_second_new, conv_new = adam_update(conv_taps, conv_first, conv_second, grad_conv, 0.3, 0.1)
    ssm_first_new, ssm_second_new, ssm_new = adam_update(ssm_params, ssm_first, ssm_second, grad_ssm, 0.8, 0.0)
    return (output.astype(jnp.bfloat16), token_grad.astype(jnp.bfloat16), in_first_new, in_second_new, in_new, dt_first_new, dt_second_new, dt_new, out_first_new, out_second_new, out_new, gu_first_new, gu_second_new, gu_new, down_first_new, down_second_new, down_new, gain_first_new, gain_second_new, gain_new, conv_first_new, conv_second_new, conv_new, ssm_first_new, ssm_second_new, ssm_new)
```

```python
import functools

import jax
import jax.numpy as jnp
from jax import lax
from jax.sharding import PartitionSpec as P

D = 1024
MIXER_HEADS = 24
MIXER_HEAD_SIZE = 64
NS = 128
QUERY_HEADS = 8
KEY_VALUE_HEADS = 2
HEAD_SIZE = 64
FF = 2048
KCONV = 4
STEP = 10
MIXER_WIDTH = 1536
CONV = 1792
NOUT = 2048


precise = lax.Precision.HIGHEST
EPSILON_NORM = 1e-05
ROPE_BASE = 10000.0
NEG_BIG = -1e30
ATT_MULT = 8.0
BETA_ONE = 0.9
BETA_TWO = 0.95
ADAM_EPS = 1e-08


def rms_scale(values, gain):
    return (
        values * lax.rsqrt(jnp.mean(values * values, axis=-1, keepdims=True) + EPSILON_NORM) * gain
    )


def layout(lengths, count_of_rows):
    seq_ends = jnp.cumsum(lengths)
    starts = seq_ends - lengths
    row_ids = jnp.arange(count_of_rows, dtype=jnp.int32)
    document = jnp.sum((row_ids[:, None] >= seq_ends[None, :]).astype(jnp.int32), axis=1)
    row_alive = row_ids < seq_ends[-1]
    slot_ids = jnp.arange(lengths.shape[0], dtype=jnp.int32)
    first_row = jnp.sum(
        jnp.where(document[:, None] == slot_ids[None, :], starts[None, :], 0), axis=1
    )
    token_position = jnp.where(row_alive, row_ids - first_row, 0)
    same_doc = (
        (document[:, None] == document[None, :])
        & row_alive[None, :]
        & (row_ids[None, :] <= row_ids[:, None])
    )
    pair_mask = same_doc | (row_ids[:, None] == row_ids[None, :])
    return (row_alive, token_position, pair_mask)


def apply_rotary(head_rows, token_position):
    half_width = head_rows.shape[-1] // 2
    frequency = ROPE_BASE ** (-jnp.arange(half_width, dtype=jnp.float32) / half_width)
    angles = token_position.astype(jnp.float32)[:, None] * frequency[None, :]
    cosine = jnp.cos(angles)[:, None, :]
    sine_part = jnp.sin(angles)[:, None, :]
    front = head_rows[..., :half_width]
    latter = head_rows[..., half_width:]
    return jnp.concatenate(
        [front * cosine - latter * sine_part, latter * cosine + front * sine_part], axis=-1
    )


def rotary_pair(query_key_pair, token_position):
    count_of_rows = query_key_pair.shape[0]
    head_rows = query_key_pair.reshape(count_of_rows, QUERY_HEADS + KEY_VALUE_HEADS, HEAD_SIZE)
    return apply_rotary(head_rows, token_position).reshape(
        count_of_rows, (QUERY_HEADS + KEY_VALUE_HEADS) * HEAD_SIZE
    )


def swiglu(gate_vals):
    return jax.nn.silu(gate_vals[:, :FF]) * gate_vals[:, FF:]


def mixer_core(zxbc, conv_weight, ssm_weight, gain_mix, pair_mask, token_position):
    count_of_rows = zxbc.shape[0]
    gate_z = zxbc[:, :MIXER_WIDTH]
    conv_in = zxbc[:, MIXER_WIDTH : MIXER_WIDTH + CONV]
    dt_raw = zxbc[:, MIXER_WIDTH + CONV : MIXER_WIDTH + CONV + MIXER_HEADS]
    conv_sum = jnp.broadcast_to(conv_weight[KCONV][None, :], conv_in.shape)
    for tap_index in range(KCONV):
        lag_rows = KCONV - 1 - tap_index
        if lag_rows == 0:
            shifted = conv_in
        else:
            shifted = jnp.concatenate(
                [jnp.zeros((lag_rows, CONV), conv_in.dtype), conv_in[: count_of_rows - lag_rows]],
                axis=0,
            )
            shifted = jnp.where((token_position >= lag_rows)[:, None], shifted, 0.0)
        conv_sum = conv_sum + conv_weight[tap_index][None, :] * shifted
    convolved_output = jax.nn.silu(conv_sum)
    input_heads = convolved_output[:, :MIXER_WIDTH].reshape(
        count_of_rows, MIXER_HEADS, MIXER_HEAD_SIZE
    )
    b_rows = convolved_output[:, MIXER_WIDTH : MIXER_WIDTH + NS]
    c_rows = convolved_output[:, MIXER_WIDTH + NS :]
    dt_step = jax.nn.softplus(dt_raw + ssm_weight[1][None, :])
    decay_rate = -jnp.exp(ssm_weight[0])
    decay_cum = jnp.cumsum(dt_step * decay_rate[None, :], axis=0).T
    decay_gaps = decay_cum[:, :, None] - decay_cum[:, None, :]
    weights = jnp.exp(jnp.where(pair_mask[None], decay_gaps, NEG_BIG))
    inner_prod = jnp.dot(c_rows, b_rows.T, precision=precise)
    kernel = weights * inner_prod[None] * dt_step.T[:, None, :]
    mixed_out = jnp.einsum("hts,shd->thd", kernel, input_heads, precision=precise)
    mixed_out = mixed_out + ssm_weight[2][None, :, None] * input_heads
    gated_out = mixed_out.reshape(count_of_rows, MIXER_WIDTH) * jax.nn.silu(gate_z)
    return rms_scale(gated_out, gain_mix)


def masked_scores(query_rows, key_reduced, pair_mask):
    scores = jnp.einsum(
        "tkgd,skd->kgts", query_rows, key_reduced, preferred_element_type=jnp.float32
    ) * HEAD_SIZE ** (-0.5)
    return jnp.where(pair_mask[None, None], scores, NEG_BIG)


def left_product(left, right):
    return lax.dot_general(
        left, right, (((0,), (0,)), ((), ())), preferred_element_type=jnp.float32
    )


def right_product(left, right):
    return lax.dot_general(
        left, right, (((1,), (1,)), ((), ())), preferred_element_type=jnp.float32
    )


def adam_update(param, first, second, grad, rate, decay):
    new_first = BETA_ONE * first + (1.0 - BETA_ONE) * grad
    new_second = BETA_TWO * second + (1.0 - BETA_TWO) * grad * grad
    first_hat = new_first / (1.0 - BETA_ONE**STEP)
    second_hat = new_second / (1.0 - BETA_TWO**STEP)
    new_param = param - rate * (first_hat / (jnp.sqrt(second_hat) + ADAM_EPS) + decay * param)
    return (new_first, new_second, new_param)


def core_halves(columns, core):
    half = columns.shape[1] // 2
    return (
        lax.dynamic_slice_in_dim(columns, core * half, half, 1),
        lax.dynamic_slice_in_dim(columns, (1 - core) * half, half, 1),
    )


def swap_cores(values, reps):
    return lax.ppermute(values, "rep", [(r, r ^ 1) for r in range(reps)])


def gather_weight(weight, core, reps):
    mine, _ = core_halves(weight.astype(jnp.bfloat16), core)
    mine = lax.all_gather(mine, "shard", axis=0, tiled=True)
    return (mine, swap_cores(mine, reps))


def forward_product(left, pair, core):
    own = jnp.dot(left, pair[0], preferred_element_type=jnp.float32)
    other = jnp.dot(left, pair[1], preferred_element_type=jnp.float32)
    low = jnp.where(core == 0, own, other)
    high = jnp.where(core == 0, other, own)
    return jnp.concatenate([low, high], axis=1)


def backward_product(left, pair, core):
    own, other = core_halves(left, core)
    return right_product(own, pair[0]) + right_product(other, pair[1])


def pair_rows(values, reps):
    return jnp.concatenate([values, swap_cores(values, reps)], axis=0)


def pair_columns(values, core, reps):
    count_of_rows, width = values.shape
    blocks = values.reshape(count_of_rows, reps // 2, 2, width // reps)
    own = lax.dynamic_index_in_dim(blocks, core, 2, False).reshape(count_of_rows, width // 2)
    other = lax.dynamic_index_in_dim(blocks, 1 - core, 2, False).reshape(count_of_rows, width // 2)
    return jnp.concatenate([own, swap_cores(other, reps)], axis=0)


def summed_block(left, right, core, reps):
    grad = left_product(pair_rows(left, reps), pair_columns(right, core, reps))
    owned = lax.psum_scatter(
        grad.astype(jnp.bfloat16), "shard", scatter_dimension=0, tiled=True
    )
    groups = [list(range(c, reps, 2)) for c in range(2)]
    block = lax.psum_scatter(
        owned, "rep", scatter_dimension=1, axis_index_groups=groups, tiled=True
    )
    return block.astype(jnp.float32)


def adam_delta(param, first, second, grad, rate, decay):
    new_first, new_second, delta = adam_update(param, first, second, grad, rate, decay)
    return (new_first, new_second, (delta - param).astype(jnp.bfloat16))


def gathered_weight(weight, delta):
    return weight + lax.all_gather(delta, "rep", axis=1, tiled=True).astype(jnp.float32)


def column_block(whole_rows, like, block_index):
    width = like.shape[1]
    return lax.dynamic_slice_in_dim(whole_rows, block_index * width, width, 1)


def local(
    reps,
    shards,
    tokens,
    cotangent,
    seq_len,
    in_proj,
    in_proj_first,
    in_proj_second,
    dt_proj,
    dt_proj_first,
    dt_proj_second,
    out_proj,
    out_proj_first,
    out_proj_second,
    gate_up,
    gate_up_first,
    gate_up_second,
    down_proj,
    down_proj_first,
    down_proj_second,
    norm_gains,
    gains_first,
    gains_second,
    conv_taps,
    conv_first,
    conv_second,
    ssm_params,
    ssm_first,
    ssm_second,
):
    rep_index = lax.axis_index("rep")
    shard_index = lax.axis_index("shard")
    core = lax.rem(rep_index, 2)
    token_local = jnp.sum(seq_len).astype(jnp.float32)
    token_count = lax.psum(token_local, ("rep", "shard"))
    small = jnp.concatenate(
        [dt_proj.reshape(-1), norm_gains.reshape(-1), conv_taps.reshape(-1)]
    ).astype(jnp.bfloat16)
    small = lax.all_gather(small, "shard", axis=0)
    dt_size, gain_size = dt_proj.size, norm_gains.size
    full_dt = small[:, :dt_size].reshape(D, MIXER_HEADS)
    full_gains = small[:, dt_size : dt_size + gain_size].reshape(-1)
    full_conv = (
        small[:, dt_size + gain_size :]
        .reshape(shards, KCONV + 1, CONV // shards)
        .transpose(1, 0, 2)
        .reshape(KCONV + 1, CONV)
    )
    full_in = gather_weight(in_proj, core, reps)
    full_out = gather_weight(out_proj, core, reps)
    full_gu = gather_weight(gate_up, core, reps)
    full_down = gather_weight(down_proj, core, reps)
    tokens, token_count = lax.optimization_barrier((tokens, token_count))
    count_of_rows = tokens.shape[0]
    row_alive, token_position, pair_mask = layout(seq_len, count_of_rows)
    inputs = tokens.astype(jnp.float32)
    gains_full = full_gains.astype(jnp.float32)
    conv_full = full_conv.astype(jnp.float32)
    normed_value, norm_back = jax.vjp(rms_scale, inputs, gains_full[:D])
    normed = normed_value.astype(jnp.bfloat16)
    main_proj = forward_product(normed, full_in, core)
    dt_raw = jnp.dot(normed, full_dt, preferred_element_type=jnp.float32)
    projected_input = jnp.concatenate(
        [main_proj[:, : MIXER_WIDTH + CONV], dt_raw, main_proj[:, MIXER_WIDTH + CONV :]], axis=1
    )
    split_boundary = MIXER_WIDTH + CONV + MIXER_HEADS
    mixer_value, mixer_back = jax.vjp(
        lambda proj_part, conv_part, ssm_part, gain_part: mixer_core(
            proj_part, conv_part, ssm_part, gain_part, pair_mask, token_position
        ),
        projected_input[:, :split_boundary],
        conv_full,
        ssm_params,
        gains_full[2 * D :],
    )
    mixer_low = mixer_value.astype(jnp.bfloat16)
    rotary_output, rope_back = jax.vjp(
        lambda query_key_pair: rotary_pair(query_key_pair, token_position),
        projected_input[
            :, split_boundary : split_boundary + (QUERY_HEADS + KEY_VALUE_HEADS) * HEAD_SIZE
        ],
    )
    query_group_width = QUERY_HEADS // KEY_VALUE_HEADS
    query_rows = (
        rotary_output[:, : QUERY_HEADS * HEAD_SIZE]
        .astype(jnp.bfloat16)
        .reshape(count_of_rows, KEY_VALUE_HEADS, query_group_width, HEAD_SIZE)
    )
    key_reduced = (
        rotary_output[:, QUERY_HEADS * HEAD_SIZE :]
        .astype(jnp.bfloat16)
        .reshape(count_of_rows, KEY_VALUE_HEADS, HEAD_SIZE)
    )
    value_reduced = (
        projected_input[:, split_boundary + (QUERY_HEADS + KEY_VALUE_HEADS) * HEAD_SIZE :]
        .astype(jnp.bfloat16)
        .reshape(count_of_rows, KEY_VALUE_HEADS, HEAD_SIZE)
    )
    scores = masked_scores(query_rows, key_reduced, pair_mask)
    log_total = jax.nn.logsumexp(scores, axis=-1, keepdims=True)
    probs_low = jnp.exp(scores - log_total).astype(jnp.bfloat16)
    attended = jnp.einsum(
        "kgts,skd->tkgd", probs_low, value_reduced, preferred_element_type=jnp.float32
    )
    attended_low = attended.reshape(count_of_rows, QUERY_HEADS * HEAD_SIZE).astype(jnp.bfloat16)
    branch_in = jnp.concatenate([mixer_low, attended_low * ATT_MULT], axis=1)
    branch = forward_product(branch_in, full_out, core)
    hidden = inputs + branch
    normed_two_value, norm_two_back = jax.vjp(rms_scale, hidden, gains_full[D : 2 * D])
    normed_two = normed_two_value.astype(jnp.bfloat16)
    gate_vals = forward_product(normed_two, full_gu, core)
    act_value, swiglu_back = jax.vjp(swiglu, gate_vals)
    act_low = act_value.astype(jnp.bfloat16)
    output = hidden + forward_product(act_low, full_down, core)
    upstream = cotangent.astype(jnp.float32) * row_alive[:, None].astype(jnp.float32)
    upstream_low = upstream.astype(jnp.bfloat16)
    summed_down = summed_block(act_low, upstream_low, core, reps)
    d_act = backward_product(upstream_low, full_down, core)
    (d_gate_vals,) = swiglu_back(d_act)
    d_gate_low = d_gate_vals.astype(jnp.bfloat16)
    summed_gu = summed_block(normed_two, d_gate_low, core, reps)
    d_normed_two = backward_product(d_gate_low, full_gu, core)
    d_hidden_norm, d_gain_two = norm_two_back(d_normed_two)
    d_hidden = upstream + d_hidden_norm
    d_branch_low = d_hidden.astype(jnp.bfloat16)
    summed_out = summed_block(branch_in, d_branch_low, core, reps)
    d_branch_in = backward_product(d_branch_low, full_out, core)
    mixer_projection_gradient, d_conv, d_ssm, d_gain_mix = mixer_back(d_branch_in[:, :MIXER_WIDTH])
    d_attended = (
        (d_branch_in[:, MIXER_WIDTH:] * ATT_MULT)
        .astype(jnp.bfloat16)
        .reshape(count_of_rows, KEY_VALUE_HEADS, query_group_width, HEAD_SIZE)
    )
    probs = jnp.exp(masked_scores(query_rows, key_reduced, pair_mask) - log_total)
    d_probs = jnp.einsum(
        "tkgd,skd->kgts", d_attended, value_reduced, preferred_element_type=jnp.float32
    )
    value_gradient = jnp.einsum(
        "kgts,tkgd->skd", probs.astype(jnp.bfloat16), d_attended, preferred_element_type=jnp.float32
    )
    row_delta = jnp.sum(probs * d_probs, axis=-1, keepdims=True)
    d_scores = (probs * (d_probs - row_delta)).astype(jnp.bfloat16)
    query_gradient = jnp.einsum(
        "kgts,skd->tkgd", d_scores, key_reduced, preferred_element_type=jnp.float32
    ) * HEAD_SIZE ** (-0.5)
    key_gradient = jnp.einsum(
        "kgts,tkgd->skd", d_scores, query_rows, preferred_element_type=jnp.float32
    ) * HEAD_SIZE ** (-0.5)
    (query_key_gradient,) = rope_back(
        jnp.concatenate(
            [
                query_gradient.reshape(count_of_rows, QUERY_HEADS * HEAD_SIZE),
                key_gradient.reshape(count_of_rows, KEY_VALUE_HEADS * HEAD_SIZE),
            ],
            axis=1,
        )
    )
    d_projected = jnp.concatenate(
        [
            mixer_projection_gradient,
            query_key_gradient,
            value_gradient.reshape(count_of_rows, KEY_VALUE_HEADS * HEAD_SIZE),
        ],
        axis=1,
    ).astype(jnp.bfloat16)
    d_main = jnp.concatenate(
        [d_projected[:, : MIXER_WIDTH + CONV], d_projected[:, split_boundary:]], axis=1
    )
    d_dt = d_projected[:, MIXER_WIDTH + CONV : split_boundary]
    summed_in = summed_block(normed, d_main, core, reps)
    grad_dt = left_product(normed, d_dt)
    d_normed = backward_product(d_main, full_in, core) + right_product(d_dt, full_dt)
    d_inputs, d_gain_one = norm_back(d_normed)
    token_grad = (d_hidden + d_inputs).astype(jnp.bfloat16)
    grad_gains = jnp.concatenate([d_gain_one, d_gain_two, d_gain_mix], axis=0)
    small_sum = lax.psum(
        jnp.concatenate(
            [grad_dt.reshape(-1), grad_gains, d_conv.reshape(-1), d_ssm.reshape(-1)]
        ),
        ("rep", "shard"),
    )
    cut_dt = grad_dt.size
    cut_gains = cut_dt + grad_gains.size
    cut_conv = cut_gains + d_conv.size
    summed_dt = lax.dynamic_slice_in_dim(small_sum[:cut_dt], shard_index * dt_size, dt_size, 0)
    summed_dt = summed_dt.reshape(dt_proj.shape)
    summed_gains = lax.dynamic_slice_in_dim(
        small_sum[cut_dt:cut_gains], shard_index * gain_size, gain_size, 0
    )
    summed_conv = lax.dynamic_slice_in_dim(
        small_sum[cut_gains:cut_conv].reshape(d_conv.shape),
        shard_index * conv_taps.shape[1],
        conv_taps.shape[1],
        1,
    )
    ssm_total = small_sum[cut_conv:].reshape(d_ssm.shape)
    in_piece = column_block(in_proj, in_proj_first, rep_index)
    out_piece = column_block(out_proj, out_proj_first, rep_index)
    gu_piece = column_block(gate_up, gate_up_first, rep_index)
    down_piece = column_block(down_proj, down_proj_first, rep_index)
    in_first_new, in_second_new, in_delta = adam_delta(
        in_piece, in_proj_first, in_proj_second, summed_in / token_count, 0.7 * D ** (-0.5), 0.1
    )
    out_first_new, out_second_new, out_delta = adam_delta(
        out_piece,
        out_proj_first,
        out_proj_second,
        summed_out / token_count,
        0.7 * NOUT ** (-0.5),
        0.1,
    )
    gu_first_new, gu_second_new, gu_delta = adam_delta(
        gu_piece, gate_up_first, gate_up_second, summed_gu / token_count, 0.7 * D ** (-0.5), 0.1
    )
    down_first_new, down_second_new, down_delta = adam_delta(
        down_piece,
        down_proj_first,
        down_proj_second,
        summed_down / token_count,
        0.7 * FF ** (-0.5),
        0.1,
    )
    down_new = gathered_weight(down_proj, down_delta)
    gu_new = gathered_weight(gate_up, gu_delta)
    out_new = gathered_weight(out_proj, out_delta)
    in_new = gathered_weight(in_proj, in_delta)
    dt_first_new, dt_second_new, dt_new = adam_update(
        dt_proj, dt_proj_first, dt_proj_second, summed_dt / token_count, 0.7 * D ** (-0.5), 0.1
    )
    gain_first_new, gain_second_new, gain_new = adam_update(
        norm_gains, gains_first, gains_second, summed_gains / token_count, 0.3, 0.0
    )
    conv_first_new, conv_second_new, conv_new = adam_update(
        conv_taps, conv_first, conv_second, summed_conv / token_count, 0.3, 0.1
    )
    ssm_first_new, ssm_second_new, ssm_new = adam_update(
        ssm_params, ssm_first, ssm_second, ssm_total / token_count, 0.8, 0.0
    )
    return (
        output.astype(jnp.bfloat16),
        token_grad,
        in_first_new,
        in_second_new,
        in_new,
        dt_first_new,
        dt_second_new,
        dt_new,
        out_first_new,
        out_second_new,
        out_new,
        gu_first_new,
        gu_second_new,
        gu_new,
        down_first_new,
        down_second_new,
        down_new,
        gain_first_new,
        gain_second_new,
        gain_new,
        conv_first_new,
        conv_second_new,
        conv_new,
        ssm_first_new,
        ssm_second_new,
        ssm_new,
    )


def solution(mesh):
    in_specs = (
        P(("rep", "shard"), None),
        P(("rep", "shard"), None),
        P(("rep", "shard")),
        P("shard", None),
        P("shard", "rep"),
        P("shard", "rep"),
        P("shard", None),
        P("shard", None),
        P("shard", None),
        P("shard", None),
        P("shard", "rep"),
        P("shard", "rep"),
        P("shard", None),
        P("shard", "rep"),
        P("shard", "rep"),
        P("shard", None),
        P("shard", "rep"),
        P("shard", "rep"),
        P("shard"),
        P("shard"),
        P("shard"),
        P(None, "shard"),
        P(None, "shard"),
        P(None, "shard"),
        P(),
        P(),
        P(),
    )
    out_specs = (
        P(("rep", "shard"), None),
        P(("rep", "shard"), None),
        P("shard", "rep"),
        P("shard", "rep"),
        P("shard", None),
        P("shard", None),
        P("shard", None),
        P("shard", None),
        P("shard", "rep"),
        P("shard", "rep"),
        P("shard", None),
        P("shard", "rep"),
        P("shard", "rep"),
        P("shard", None),
        P("shard", "rep"),
        P("shard", "rep"),
        P("shard", None),
        P("shard"),
        P("shard"),
        P("shard"),
        P(None, "shard"),
        P(None, "shard"),
        P(None, "shard"),
        P(),
        P(),
        P(),
    )
    step = functools.partial(local, mesh.shape["rep"], mesh.shape["shard"])
    return jax.shard_map(step, mesh=mesh, in_specs=in_specs, out_specs=out_specs, check_vma=False)
```

```python
import functools

import jax
import jax.numpy as jnp
from jax import lax
from jax.sharding import PartitionSpec as P

D = 1024
MIXER_HEADS = 24
MIXER_HEAD_SIZE = 64
NS = 128
QUERY_HEADS = 8
KEY_VALUE_HEADS = 2
HEAD_SIZE = 64
FF = 2048
KCONV = 4
STEP = 10
MIXER_WIDTH = 1536
CONV = 1792
NOUT = 2048


precise = lax.Precision.HIGHEST
EPSILON_NORM = 1e-05
ROPE_BASE = 10000.0
NEG_BIG = -1e30
ATT_MULT = 8.0
BETA_ONE = 0.9
BETA_TWO = 0.95
ADAM_EPS = 1e-08


def rms_scale(values, gain):
    return (
        values * lax.rsqrt(jnp.mean(values * values, axis=-1, keepdims=True) + EPSILON_NORM) * gain
    )


def layout(lengths, count_of_rows):
    seq_ends = jnp.cumsum(lengths)
    starts = seq_ends - lengths
    row_ids = jnp.arange(count_of_rows, dtype=jnp.int32)
    document = jnp.sum((row_ids[:, None] >= seq_ends[None, :]).astype(jnp.int32), axis=1)
    row_alive = row_ids < seq_ends[-1]
    slot_ids = jnp.arange(lengths.shape[0], dtype=jnp.int32)
    first_row = jnp.sum(
        jnp.where(document[:, None] == slot_ids[None, :], starts[None, :], 0), axis=1
    )
    token_position = jnp.where(row_alive, row_ids - first_row, 0)
    same_doc = (
        (document[:, None] == document[None, :])
        & row_alive[None, :]
        & (row_ids[None, :] <= row_ids[:, None])
    )
    pair_mask = same_doc | (row_ids[:, None] == row_ids[None, :])
    return (row_alive, token_position, pair_mask)


def apply_rotary(head_rows, token_position):
    half_width = head_rows.shape[-1] // 2
    frequency = ROPE_BASE ** (-jnp.arange(half_width, dtype=jnp.float32) / half_width)
    angles = token_position.astype(jnp.float32)[:, None] * frequency[None, :]
    cosine = jnp.cos(angles)[:, None, :]
    sine_part = jnp.sin(angles)[:, None, :]
    front = head_rows[..., :half_width]
    latter = head_rows[..., half_width:]
    return jnp.concatenate(
        [front * cosine - latter * sine_part, latter * cosine + front * sine_part], axis=-1
    )


def rotary_pair(query_key_pair, token_position):
    count_of_rows = query_key_pair.shape[0]
    head_rows = query_key_pair.reshape(count_of_rows, QUERY_HEADS + KEY_VALUE_HEADS, HEAD_SIZE)
    return apply_rotary(head_rows, token_position).reshape(
        count_of_rows, (QUERY_HEADS + KEY_VALUE_HEADS) * HEAD_SIZE
    )


def swiglu(gate_vals):
    return jax.nn.silu(gate_vals[:, :FF]) * gate_vals[:, FF:]


def mixer_core(zxbc, conv_weight, ssm_weight, gain_mix, pair_mask, token_position):
    count_of_rows = zxbc.shape[0]
    gate_z = zxbc[:, :MIXER_WIDTH]
    conv_in = zxbc[:, MIXER_WIDTH : MIXER_WIDTH + CONV]
    dt_raw = zxbc[:, MIXER_WIDTH + CONV : MIXER_WIDTH + CONV + MIXER_HEADS]
    conv_sum = jnp.broadcast_to(conv_weight[KCONV][None, :], conv_in.shape)
    for tap_index in range(KCONV):
        lag_rows = KCONV - 1 - tap_index
        if lag_rows == 0:
            shifted = conv_in
        else:
            shifted = jnp.concatenate(
                [jnp.zeros((lag_rows, CONV), conv_in.dtype), conv_in[: count_of_rows - lag_rows]],
                axis=0,
            )
            shifted = jnp.where((token_position >= lag_rows)[:, None], shifted, 0.0)
        conv_sum = conv_sum + conv_weight[tap_index][None, :] * shifted
    convolved_output = jax.nn.silu(conv_sum)
    input_heads = convolved_output[:, :MIXER_WIDTH].reshape(
        count_of_rows, MIXER_HEADS, MIXER_HEAD_SIZE
    )
    b_rows = convolved_output[:, MIXER_WIDTH : MIXER_WIDTH + NS]
    c_rows = convolved_output[:, MIXER_WIDTH + NS :]
    dt_step = jax.nn.softplus(dt_raw + ssm_weight[1][None, :])
    decay_rate = -jnp.exp(ssm_weight[0])
    decay_cum = jnp.cumsum(dt_step * decay_rate[None, :], axis=0).T
    decay_gaps = decay_cum[:, :, None] - decay_cum[:, None, :]
    weights = jnp.exp(jnp.where(pair_mask[None], decay_gaps, NEG_BIG))
    inner_prod = jnp.dot(c_rows, b_rows.T, precision=precise)
    kernel = weights * inner_prod[None] * dt_step.T[:, None, :]
    mixed_out = jnp.einsum("hts,shd->thd", kernel, input_heads, precision=precise)
    mixed_out = mixed_out + ssm_weight[2][None, :, None] * input_heads
    gated_out = mixed_out.reshape(count_of_rows, MIXER_WIDTH) * jax.nn.silu(gate_z)
    return rms_scale(gated_out, gain_mix)


def masked_scores(query_rows, key_reduced, pair_mask):
    scores = jnp.einsum(
        "tkgd,skd->kgts", query_rows, key_reduced, preferred_element_type=jnp.float32
    ) * HEAD_SIZE ** (-0.5)
    return jnp.where(pair_mask[None, None], scores, NEG_BIG)


def left_product(left, right):
    return lax.dot_general(
        left, right, (((0,), (0,)), ((), ())), preferred_element_type=jnp.float32
    )


def right_product(left, right):
    return lax.dot_general(
        left, right, (((1,), (1,)), ((), ())), preferred_element_type=jnp.float32
    )


def adam_update(param, first, second, grad, rate, decay):
    new_first = BETA_ONE * first + (1.0 - BETA_ONE) * grad
    new_second = BETA_TWO * second + (1.0 - BETA_TWO) * grad * grad
    first_hat = new_first / (1.0 - BETA_ONE**STEP)
    second_hat = new_second / (1.0 - BETA_TWO**STEP)
    new_param = param - rate * (first_hat / (jnp.sqrt(second_hat) + ADAM_EPS) + decay * param)
    return (new_first, new_second, new_param)


def core_halves(columns, core):
    half = columns.shape[1] // 2
    return (
        lax.dynamic_slice_in_dim(columns, core * half, half, 1),
        lax.dynamic_slice_in_dim(columns, (1 - core) * half, half, 1),
    )


def swap_cores(values, reps):
    return lax.ppermute(values, "rep", [(r, r ^ 1) for r in range(reps)])


def own_half(weight, core):
    return core_halves(weight.astype(jnp.bfloat16), core)[0]


def with_swapped(own, reps):
    return (own, swap_cores(own, reps))


def stack_columns(block, width):
    rows, columns = block.shape
    return block.reshape(rows, columns // width, width).transpose(1, 0, 2).reshape(-1, width)


def unstack_columns(stacked, rows):
    width = stacked.shape[-1]
    blocks = stacked.reshape(-1, rows, width)
    return blocks.transpose(1, 0, 2).reshape(rows, -1)


def unstack_gathered(stacked, rows):
    parts, _, width = stacked.shape
    blocks = stacked.reshape(parts, -1, rows, width)
    return blocks.transpose(0, 2, 1, 3).reshape(parts * rows, -1)


def total_over_mesh(values, reps, shards):
    for axis, size in (("rep", reps), ("shard", shards)):
        step = 1
        while step < size:
            values = values + lax.ppermute(values, axis, [(i, i ^ step) for i in range(size)])
            step *= 2
    return values


def forward_product(left, pair, core):
    own = jnp.dot(left, pair[0], preferred_element_type=jnp.float32)
    other = jnp.dot(left, pair[1], preferred_element_type=jnp.float32)
    low = jnp.where(core == 0, own, other)
    high = jnp.where(core == 0, other, own)
    return jnp.concatenate([low, high], axis=1)


def backward_product(left, pair, core):
    own, other = core_halves(left, core)
    return right_product(own, pair[0]) + right_product(other, pair[1])


def pair_rows(values, reps):
    return jnp.concatenate([values, swap_cores(values, reps)], axis=0)


def pair_columns(values, core, reps):
    count_of_rows, width = values.shape
    blocks = values.reshape(count_of_rows, reps // 2, 2, width // reps)
    own = lax.dynamic_index_in_dim(blocks, core, 2, False).reshape(count_of_rows, width // 2)
    other = lax.dynamic_index_in_dim(blocks, 1 - core, 2, False).reshape(count_of_rows, width // 2)
    return jnp.concatenate([own, swap_cores(other, reps)], axis=0)


def pair_gradient(left, right, core, reps):
    grad = left_product(pair_rows(left, reps), pair_columns(right, core, reps))
    return grad.astype(jnp.bfloat16)


def packed_blocks(grads, shards, lane):
    stacked = []
    for grad in grads:
        rows = grad.shape[0] // shards
        blocks = grad.reshape(shards, rows, -1, lane).transpose(0, 2, 1, 3)
        stacked.append(blocks.reshape(shards, -1, lane))
    return jnp.concatenate(stacked, axis=1).reshape(-1, lane)


def owned_blocks(packed, like, reps):
    owned = lax.psum_scatter(packed, "shard", scatter_dimension=0, tiled=True)
    lane = owned.shape[1]
    cut = like.size // 2 // lane
    return [part.reshape(reps // 2, -1, lane) for part in (owned[:cut], owned[cut:])]


def adam_delta(param, first, second, grad, rate, decay):
    new_first, new_second, delta = adam_update(param, first, second, grad, rate, decay)
    return (new_first, new_second, (delta - param).astype(jnp.bfloat16))


def column_block(whole_rows, like, block_index):
    width = like.shape[1]
    return lax.dynamic_slice_in_dim(whole_rows, block_index * width, width, 1)


def local(
    reps,
    shards,
    tokens,
    cotangent,
    seq_len,
    in_proj,
    in_proj_first,
    in_proj_second,
    dt_proj,
    dt_proj_first,
    dt_proj_second,
    out_proj,
    out_proj_first,
    out_proj_second,
    gate_up,
    gate_up_first,
    gate_up_second,
    down_proj,
    down_proj_first,
    down_proj_second,
    norm_gains,
    gains_first,
    gains_second,
    conv_taps,
    conv_first,
    conv_second,
    ssm_params,
    ssm_first,
    ssm_second,
):
    rep_index = lax.axis_index("rep")
    shard_index = lax.axis_index("shard")
    core = lax.rem(rep_index, 2)
    lane = min(128, out_proj_first.shape[1])
    token_local = jnp.sum(seq_len).astype(jnp.float32)
    low_in = lax.all_gather(own_half(in_proj, core), "shard", axis=0, tiled=True)
    full_in = with_swapped(low_in, reps)
    small = jnp.concatenate(
        [dt_proj.reshape(-1), norm_gains.reshape(-1), conv_taps.reshape(-1)]
    ).astype(jnp.bfloat16)
    small = lax.all_gather(small, "shard", axis=0)
    dt_size, gain_size = dt_proj.size, norm_gains.size
    full_dt = small[:, :dt_size].reshape(D, MIXER_HEADS)
    full_gains = small[:, dt_size : dt_size + gain_size].reshape(-1)
    full_conv = (
        small[:, dt_size + gain_size :]
        .reshape(shards, KCONV + 1, CONV // shards)
        .transpose(1, 0, 2)
        .reshape(KCONV + 1, CONV)
    )
    width = out_proj.shape[1] // 2
    rest_parts = [
        own_half(out_proj, core),
        stack_columns(own_half(gate_up, core), width),
        own_half(down_proj, core),
    ]
    rest_cuts = (rest_parts[0].shape[0], rest_parts[0].shape[0] + rest_parts[1].shape[0])
    rest = lax.all_gather(jnp.concatenate(rest_parts, axis=0), "shard", axis=0)
    count_of_rows = tokens.shape[0]
    row_alive, token_position, pair_mask = layout(seq_len, count_of_rows)
    inputs = tokens.astype(jnp.float32)
    gains_full = full_gains.astype(jnp.float32)
    conv_full = full_conv.astype(jnp.float32)
    normed_value, norm_back = jax.vjp(rms_scale, inputs, gains_full[:D])
    normed = normed_value.astype(jnp.bfloat16)
    main_proj = forward_product(normed, full_in, core)
    dt_raw = jnp.dot(normed, full_dt, preferred_element_type=jnp.float32)
    projected_input = jnp.concatenate(
        [main_proj[:, : MIXER_WIDTH + CONV], dt_raw, main_proj[:, MIXER_WIDTH + CONV :]], axis=1
    )
    split_boundary = MIXER_WIDTH + CONV + MIXER_HEADS
    mixer_value, mixer_back = jax.vjp(
        lambda proj_part, conv_part, ssm_part, gain_part: mixer_core(
            proj_part, conv_part, ssm_part, gain_part, pair_mask, token_position
        ),
        projected_input[:, :split_boundary],
        conv_full,
        ssm_params,
        gains_full[2 * D :],
    )
    mixer_low = mixer_value.astype(jnp.bfloat16)
    rotary_output, rope_back = jax.vjp(
        lambda query_key_pair: rotary_pair(query_key_pair, token_position),
        projected_input[
            :, split_boundary : split_boundary + (QUERY_HEADS + KEY_VALUE_HEADS) * HEAD_SIZE
        ],
    )
    query_group_width = QUERY_HEADS // KEY_VALUE_HEADS
    query_rows = (
        rotary_output[:, : QUERY_HEADS * HEAD_SIZE]
        .astype(jnp.bfloat16)
        .reshape(count_of_rows, KEY_VALUE_HEADS, query_group_width, HEAD_SIZE)
    )
    key_reduced = (
        rotary_output[:, QUERY_HEADS * HEAD_SIZE :]
        .astype(jnp.bfloat16)
        .reshape(count_of_rows, KEY_VALUE_HEADS, HEAD_SIZE)
    )
    value_reduced = (
        projected_input[:, split_boundary + (QUERY_HEADS + KEY_VALUE_HEADS) * HEAD_SIZE :]
        .astype(jnp.bfloat16)
        .reshape(count_of_rows, KEY_VALUE_HEADS, HEAD_SIZE)
    )
    scores = masked_scores(query_rows, key_reduced, pair_mask)
    log_total = jax.nn.logsumexp(scores, axis=-1, keepdims=True)
    probs_low = jnp.exp(scores - log_total).astype(jnp.bfloat16)
    attended = jnp.einsum(
        "kgts,skd->tkgd", probs_low, value_reduced, preferred_element_type=jnp.float32
    )
    attended_low = attended.reshape(count_of_rows, QUERY_HEADS * HEAD_SIZE).astype(jnp.bfloat16)
    branch_in = jnp.concatenate([mixer_low, attended_low * ATT_MULT], axis=1)
    rest, branch_in = lax.optimization_barrier((rest, branch_in))
    full_out = with_swapped(unstack_gathered(rest[:, : rest_cuts[0]], out_proj.shape[0]), reps)
    full_gu = with_swapped(
        unstack_gathered(rest[:, rest_cuts[0] : rest_cuts[1]], gate_up.shape[0]), reps
    )
    full_down = with_swapped(unstack_gathered(rest[:, rest_cuts[1] :], down_proj.shape[0]), reps)
    branch = forward_product(branch_in, full_out, core)
    hidden = inputs + branch
    normed_two_value, norm_two_back = jax.vjp(rms_scale, hidden, gains_full[D : 2 * D])
    normed_two = normed_two_value.astype(jnp.bfloat16)
    gate_vals = forward_product(normed_two, full_gu, core)
    act_value, swiglu_back = jax.vjp(swiglu, gate_vals)
    act_low = act_value.astype(jnp.bfloat16)
    output = hidden + forward_product(act_low, full_down, core)
    upstream = cotangent.astype(jnp.float32) * row_alive[:, None].astype(jnp.float32)
    upstream_low = upstream.astype(jnp.bfloat16)
    grad_down = pair_gradient(act_low, upstream_low, core, reps)
    d_act = backward_product(upstream_low, full_down, core)
    (d_gate_vals,) = swiglu_back(d_act)
    d_gate_low = d_gate_vals.astype(jnp.bfloat16)
    grad_gu = pair_gradient(normed_two, d_gate_low, core, reps)
    d_normed_two = backward_product(d_gate_low, full_gu, core)
    d_hidden_norm, d_gain_two = norm_two_back(d_normed_two)
    d_hidden = upstream + d_hidden_norm
    d_branch_low = d_hidden.astype(jnp.bfloat16)
    packed = packed_blocks((grad_down, grad_gu), shards, lane)
    packed, d_branch_low = lax.optimization_barrier((packed, d_branch_low))
    owned_down, owned_gu = owned_blocks(packed, down_proj, reps)
    grad_out = pair_gradient(branch_in, d_branch_low, core, reps)
    d_branch_in = backward_product(d_branch_low, full_out, core)
    mixer_projection_gradient, d_conv, d_ssm, d_gain_mix = mixer_back(d_branch_in[:, :MIXER_WIDTH])
    d_attended = (
        (d_branch_in[:, MIXER_WIDTH:] * ATT_MULT)
        .astype(jnp.bfloat16)
        .reshape(count_of_rows, KEY_VALUE_HEADS, query_group_width, HEAD_SIZE)
    )
    probs = jnp.exp(masked_scores(query_rows, key_reduced, pair_mask) - log_total)
    d_probs = jnp.einsum(
        "tkgd,skd->kgts", d_attended, value_reduced, preferred_element_type=jnp.float32
    )
    value_gradient = jnp.einsum(
        "kgts,tkgd->skd", probs.astype(jnp.bfloat16), d_attended, preferred_element_type=jnp.float32
    )
    row_delta = jnp.sum(probs * d_probs, axis=-1, keepdims=True)
    d_scores = (probs * (d_probs - row_delta)).astype(jnp.bfloat16)
    query_gradient = jnp.einsum(
        "kgts,skd->tkgd", d_scores, key_reduced, preferred_element_type=jnp.float32
    ) * HEAD_SIZE ** (-0.5)
    key_gradient = jnp.einsum(
        "kgts,tkgd->skd", d_scores, query_rows, preferred_element_type=jnp.float32
    ) * HEAD_SIZE ** (-0.5)
    (query_key_gradient,) = rope_back(
        jnp.concatenate(
            [
                query_gradient.reshape(count_of_rows, QUERY_HEADS * HEAD_SIZE),
                key_gradient.reshape(count_of_rows, KEY_VALUE_HEADS * HEAD_SIZE),
            ],
            axis=1,
        )
    )
    d_projected = jnp.concatenate(
        [
            mixer_projection_gradient,
            query_key_gradient,
            value_gradient.reshape(count_of_rows, KEY_VALUE_HEADS * HEAD_SIZE),
        ],
        axis=1,
    ).astype(jnp.bfloat16)
    d_main = jnp.concatenate(
        [d_projected[:, : MIXER_WIDTH + CONV], d_projected[:, split_boundary:]], axis=1
    )
    d_dt = d_projected[:, MIXER_WIDTH + CONV : split_boundary]
    grad_in = pair_gradient(normed, d_main, core, reps)
    packed = packed_blocks((grad_out, grad_in), shards, lane)
    packed, d_main, d_dt = lax.optimization_barrier((packed, d_main, d_dt))
    owned_out, owned_in = owned_blocks(packed, out_proj, reps)
    grad_dt = left_product(normed, d_dt)
    d_normed = backward_product(d_main, full_in, core) + right_product(d_dt, full_dt)
    d_inputs, d_gain_one = norm_back(d_normed)
    token_grad = (d_hidden + d_inputs).astype(jnp.bfloat16)
    grad_gains = jnp.concatenate([d_gain_one, d_gain_two, d_gain_mix], axis=0)
    small_sum = total_over_mesh(
        jnp.concatenate(
            [
                grad_dt.reshape(-1),
                grad_gains,
                d_conv.reshape(-1),
                d_ssm.reshape(-1),
                token_local[None],
            ]
        ),
        reps,
        shards,
    )
    owned = (owned_down, owned_gu, owned_out, owned_in)
    owned, small_sum = lax.optimization_barrier((owned, small_sum))
    groups = [list(range(c, reps, 2)) for c in range(2)]
    summed = lax.psum_scatter(
        jnp.concatenate(owned, axis=1).reshape(-1, lane),
        "rep",
        scatter_dimension=0,
        axis_index_groups=groups,
        tiled=True,
    ).astype(jnp.float32)
    piece_cuts = [0]
    for part in owned:
        piece_cuts.append(piece_cuts[-1] + part.shape[1])
    summed_down, summed_gu, summed_out, summed_in = [
        unstack_columns(summed[piece_cuts[i] : piece_cuts[i + 1]], like.shape[0])
        for i, like in enumerate((down_proj, gate_up, out_proj, in_proj))
    ]
    cut_dt = grad_dt.size
    cut_gains = cut_dt + grad_gains.size
    cut_conv = cut_gains + d_conv.size
    summed_dt = lax.dynamic_slice_in_dim(small_sum[:cut_dt], shard_index * dt_size, dt_size, 0)
    summed_dt = summed_dt.reshape(dt_proj.shape)
    summed_gains = lax.dynamic_slice_in_dim(
        small_sum[cut_dt:cut_gains], shard_index * gain_size, gain_size, 0
    )
    summed_conv = lax.dynamic_slice_in_dim(
        small_sum[cut_gains:cut_conv].reshape(d_conv.shape),
        shard_index * conv_taps.shape[1],
        conv_taps.shape[1],
        1,
    )
    ssm_total = small_sum[cut_conv:-1].reshape(d_ssm.shape)
    token_count = small_sum[-1]
    in_piece = column_block(in_proj, in_proj_first, rep_index)
    out_piece = column_block(out_proj, out_proj_first, rep_index)
    gu_piece = column_block(gate_up, gate_up_first, rep_index)
    down_piece = column_block(down_proj, down_proj_first, rep_index)
    in_first_new, in_second_new, in_delta = adam_delta(
        in_piece, in_proj_first, in_proj_second, summed_in / token_count, 0.7 * D ** (-0.5), 0.1
    )
    out_first_new, out_second_new, out_delta = adam_delta(
        out_piece,
        out_proj_first,
        out_proj_second,
        summed_out / token_count,
        0.7 * NOUT ** (-0.5),
        0.1,
    )
    gu_first_new, gu_second_new, gu_delta = adam_delta(
        gu_piece, gate_up_first, gate_up_second, summed_gu / token_count, 0.7 * D ** (-0.5), 0.1
    )
    down_first_new, down_second_new, down_delta = adam_delta(
        down_piece,
        down_proj_first,
        down_proj_second,
        summed_down / token_count,
        0.7 * FF ** (-0.5),
        0.1,
    )
    deltas = lax.all_gather(
        jnp.concatenate(
            [stack_columns(delta, lane) for delta in (down_delta, gu_delta, out_delta, in_delta)],
            axis=0,
        ),
        "rep",
        axis=0,
    )
    down_new, gu_new, out_new, in_new = [
        weight
        + unstack_columns(
            deltas[:, piece_cuts[i] : piece_cuts[i + 1]], weight.shape[0]
        ).astype(jnp.float32)
        for i, weight in enumerate((down_proj, gate_up, out_proj, in_proj))
    ]
    dt_first_new, dt_second_new, dt_new = adam_update(
        dt_proj, dt_proj_first, dt_proj_second, summed_dt / token_count, 0.7 * D ** (-0.5), 0.1
    )
    gain_first_new, gain_second_new, gain_new = adam_update(
        norm_gains, gains_first, gains_second, summed_gains / token_count, 0.3, 0.0
    )
    conv_first_new, conv_second_new, conv_new = adam_update(
        conv_taps, conv_first, conv_second, summed_conv / token_count, 0.3, 0.1
    )
    ssm_first_new, ssm_second_new, ssm_new = adam_update(
        ssm_params, ssm_first, ssm_second, ssm_total / token_count, 0.8, 0.0
    )
    return (
        output.astype(jnp.bfloat16),
        token_grad,
        in_first_new,
        in_second_new,
        in_new,
        dt_first_new,
        dt_second_new,
        dt_new,
        out_first_new,
        out_second_new,
        out_new,
        gu_first_new,
        gu_second_new,
        gu_new,
        down_first_new,
        down_second_new,
        down_new,
        gain_first_new,
        gain_second_new,
        gain_new,
        conv_first_new,
        conv_second_new,
        conv_new,
        ssm_first_new,
        ssm_second_new,
        ssm_new,
    )


def solution(mesh):
    in_specs = (
        P(("rep", "shard"), None),
        P(("rep", "shard"), None),
        P(("rep", "shard")),
        P("shard", None),
        P("shard", "rep"),
        P("shard", "rep"),
        P("shard", None),
        P("shard", None),
        P("shard", None),
        P("shard", None),
        P("shard", "rep"),
        P("shard", "rep"),
        P("shard", None),
        P("shard", "rep"),
        P("shard", "rep"),
        P("shard", None),
        P("shard", "rep"),
        P("shard", "rep"),
        P("shard"),
        P("shard"),
        P("shard"),
        P(None, "shard"),
        P(None, "shard"),
        P(None, "shard"),
        P(),
        P(),
        P(),
    )
    out_specs = (
        P(("rep", "shard"), None),
        P(("rep", "shard"), None),
        P("shard", "rep"),
        P("shard", "rep"),
        P("shard", None),
        P("shard", None),
        P("shard", None),
        P("shard", None),
        P("shard", "rep"),
        P("shard", "rep"),
        P("shard", None),
        P("shard", "rep"),
        P("shard", "rep"),
        P("shard", None),
        P("shard", "rep"),
        P("shard", "rep"),
        P("shard", None),
        P("shard"),
        P("shard"),
        P("shard"),
        P(None, "shard"),
        P(None, "shard"),
        P(None, "shard"),
        P(),
        P(),
        P(),
    )
    step = functools.partial(local, mesh.shape["rep"], mesh.shape["shard"])
    return jax.shard_map(step, mesh=mesh, in_specs=in_specs, out_specs=out_specs, check_vma=False)
```

```python
import functools

import jax
import jax.numpy as jnp
from jax import lax
from jax.experimental.layout import Layout, with_layout_constraint
from jax.sharding import PartitionSpec as P

D = 1024
MIXER_HEADS = 24
MIXER_HEAD_SIZE = 64
NS = 128
QUERY_HEADS = 8
KEY_VALUE_HEADS = 2
HEAD_SIZE = 64
FF = 2048
KCONV = 4
STEP = 10
MIXER_WIDTH = 1536
CONV = 1792
NOUT = 2048


precise = lax.Precision.HIGHEST
EPSILON_NORM = 1e-05
ROPE_BASE = 10000.0
NEG_BIG = -1e30
ATT_MULT = 8.0
BETA_ONE = 0.9
BETA_TWO = 0.95
ADAM_EPS = 1e-08


def rms_scale(values, gain):
    return (
        values * lax.rsqrt(jnp.mean(values * values, axis=-1, keepdims=True) + EPSILON_NORM) * gain
    )


def layout(lengths, count_of_rows):
    seq_ends = jnp.cumsum(lengths)
    starts = seq_ends - lengths
    row_ids = jnp.arange(count_of_rows, dtype=jnp.int32)
    document = jnp.sum((row_ids[:, None] >= seq_ends[None, :]).astype(jnp.int32), axis=1)
    row_alive = row_ids < seq_ends[-1]
    slot_ids = jnp.arange(lengths.shape[0], dtype=jnp.int32)
    first_row = jnp.sum(
        jnp.where(document[:, None] == slot_ids[None, :], starts[None, :], 0), axis=1
    )
    token_position = jnp.where(row_alive, row_ids - first_row, 0)
    same_doc = (
        (document[:, None] == document[None, :])
        & row_alive[None, :]
        & (row_ids[None, :] <= row_ids[:, None])
    )
    pair_mask = same_doc | (row_ids[:, None] == row_ids[None, :])
    return (row_alive, token_position, pair_mask)


def apply_rotary(head_rows, token_position):
    half_width = head_rows.shape[-1] // 2
    frequency = ROPE_BASE ** (-jnp.arange(half_width, dtype=jnp.float32) / half_width)
    angles = token_position.astype(jnp.float32)[:, None] * frequency[None, :]
    cosine = jnp.cos(angles)[:, None, :]
    sine_part = jnp.sin(angles)[:, None, :]
    front = head_rows[..., :half_width]
    latter = head_rows[..., half_width:]
    return jnp.concatenate(
        [front * cosine - latter * sine_part, latter * cosine + front * sine_part], axis=-1
    )


def rotary_pair(query_key_pair, token_position):
    count_of_rows = query_key_pair.shape[0]
    head_rows = query_key_pair.reshape(count_of_rows, QUERY_HEADS + KEY_VALUE_HEADS, HEAD_SIZE)
    return apply_rotary(head_rows, token_position).reshape(
        count_of_rows, (QUERY_HEADS + KEY_VALUE_HEADS) * HEAD_SIZE
    )


def swiglu(gate_vals):
    return jax.nn.silu(gate_vals[:, :FF]) * gate_vals[:, FF:]


def mixer_core(zxbc, conv_weight, ssm_weight, gain_mix, pair_mask, token_position):
    count_of_rows = zxbc.shape[0]
    gate_z = zxbc[:, :MIXER_WIDTH]
    conv_in = zxbc[:, MIXER_WIDTH : MIXER_WIDTH + CONV]
    dt_raw = zxbc[:, MIXER_WIDTH + CONV : MIXER_WIDTH + CONV + MIXER_HEADS]
    conv_sum = jnp.broadcast_to(conv_weight[KCONV][None, :], conv_in.shape)
    for tap_index in range(KCONV):
        lag_rows = KCONV - 1 - tap_index
        if lag_rows == 0:
            shifted = conv_in
        else:
            shifted = jnp.concatenate(
                [jnp.zeros((lag_rows, CONV), conv_in.dtype), conv_in[: count_of_rows - lag_rows]],
                axis=0,
            )
            shifted = jnp.where((token_position >= lag_rows)[:, None], shifted, 0.0)
        conv_sum = conv_sum + conv_weight[tap_index][None, :] * shifted
    convolved_output = jax.nn.silu(conv_sum)
    input_heads = convolved_output[:, :MIXER_WIDTH].reshape(
        count_of_rows, MIXER_HEADS, MIXER_HEAD_SIZE
    )
    b_rows = convolved_output[:, MIXER_WIDTH : MIXER_WIDTH + NS]
    c_rows = convolved_output[:, MIXER_WIDTH + NS :]
    dt_step = jax.nn.softplus(dt_raw + ssm_weight[1][None, :])
    decay_rate = -jnp.exp(ssm_weight[0])
    decay_cum = jnp.cumsum(dt_step * decay_rate[None, :], axis=0).T
    decay_gaps = decay_cum[:, :, None] - decay_cum[:, None, :]
    weights = jnp.exp(jnp.where(pair_mask[None], decay_gaps, NEG_BIG))
    inner_prod = jnp.dot(c_rows, b_rows.T, precision=precise)
    kernel = weights * inner_prod[None] * dt_step.T[:, None, :]
    mixed_out = jnp.einsum("hts,shd->thd", kernel, input_heads, precision=precise)
    mixed_out = mixed_out + ssm_weight[2][None, :, None] * input_heads
    gated_out = mixed_out.reshape(count_of_rows, MIXER_WIDTH) * jax.nn.silu(gate_z)
    return rms_scale(gated_out, gain_mix)


def masked_scores(query_rows, key_reduced, pair_mask):
    scores = jnp.einsum(
        "tkgd,skd->kgts", query_rows, key_reduced, preferred_element_type=jnp.float32
    ) * HEAD_SIZE ** (-0.5)
    return jnp.where(pair_mask[None, None], scores, NEG_BIG)


def left_product(left, right):
    return lax.dot_general(
        left, right, (((0,), (0,)), ((), ())), preferred_element_type=jnp.float32
    )


def right_product(left, right):
    return lax.dot_general(
        left, right, (((1,), (1,)), ((), ())), preferred_element_type=jnp.float32
    )


def adam_update(param, first, second, grad, rate, decay):
    new_first = BETA_ONE * first + (1.0 - BETA_ONE) * grad
    new_second = BETA_TWO * second + (1.0 - BETA_TWO) * grad * grad
    first_hat = new_first / (1.0 - BETA_ONE**STEP)
    second_hat = new_second / (1.0 - BETA_TWO**STEP)
    new_param = param - rate * (first_hat / (jnp.sqrt(second_hat) + ADAM_EPS) + decay * param)
    return (new_first, new_second, new_param)


def core_halves(columns, core):
    half = columns.shape[1] // 2
    return (
        lax.dynamic_slice_in_dim(columns, core * half, half, 1),
        lax.dynamic_slice_in_dim(columns, (1 - core) * half, half, 1),
    )


def swap_cores(values, reps):
    return lax.ppermute(values, "rep", [(r, r ^ 1) for r in range(reps)])


def own_half(weight, core):
    return core_halves(weight.astype(jnp.bfloat16), core)[0]


def with_swapped(own, reps):
    return (own, swap_cores(own, reps))


def row_major(values):
    return with_layout_constraint(values, Layout(major_to_minor=(0, 1)))


def stack_columns(block, width):
    block = row_major(block)
    rows, columns = block.shape
    return block.reshape(rows, columns // width, width).transpose(1, 0, 2).reshape(-1, width)


def unstack_columns(stacked, rows):
    width = stacked.shape[-1]
    blocks = stacked.reshape(-1, rows, width)
    return row_major(blocks.transpose(1, 0, 2).reshape(rows, -1))


def unstack_gathered(stacked, rows):
    parts, _, width = stacked.shape
    blocks = stacked.reshape(parts, -1, rows, width)
    return row_major(blocks.transpose(0, 2, 1, 3).reshape(parts * rows, -1))


def total_over_mesh(values, reps, shards):
    for axis, size in (("rep", reps), ("shard", shards)):
        step = 1
        while step < size:
            values = values + lax.ppermute(values, axis, [(i, i ^ step) for i in range(size)])
            step *= 2
    return values


def forward_product(left, pair, core):
    own = jnp.dot(left, pair[0], preferred_element_type=jnp.float32)
    other = jnp.dot(left, pair[1], preferred_element_type=jnp.float32)
    low = jnp.where(core == 0, own, other)
    high = jnp.where(core == 0, other, own)
    return jnp.concatenate([low, high], axis=1)


def backward_product(left, pair, core):
    own, other = core_halves(left, core)
    return right_product(own, pair[0]) + right_product(other, pair[1])


def pair_rows(values, reps):
    return jnp.concatenate([values, swap_cores(values, reps)], axis=0)


def pair_columns(values, core, reps):
    count_of_rows, width = values.shape
    blocks = values.reshape(count_of_rows, reps // 2, 2, width // reps)
    own = lax.dynamic_index_in_dim(blocks, core, 2, False).reshape(count_of_rows, width // 2)
    other = lax.dynamic_index_in_dim(blocks, 1 - core, 2, False).reshape(count_of_rows, width // 2)
    return jnp.concatenate([own, swap_cores(other, reps)], axis=0)


def pair_gradient(left, right, core, reps):
    grad = left_product(pair_rows(left, reps), pair_columns(right, core, reps))
    return grad.astype(jnp.bfloat16)


def packed_blocks(grads, shards, lane):
    stacked = []
    for grad in grads:
        rows = grad.shape[0] // shards
        blocks = grad.reshape(shards, rows, -1, lane).transpose(0, 2, 1, 3)
        stacked.append(blocks.reshape(shards, -1, lane))
    return jnp.concatenate(stacked, axis=1).reshape(-1, lane)


def owned_blocks(packed, like, reps):
    owned = lax.psum_scatter(packed, "shard", scatter_dimension=0, tiled=True)
    lane = owned.shape[1]
    cut = like.size // 2 // lane
    return [part.reshape(reps // 2, -1, lane) for part in (owned[:cut], owned[cut:])]


def adam_delta(param, first, second, grad, rate, decay):
    new_first, new_second, delta = adam_update(param, first, second, grad, rate, decay)
    return (new_first, new_second, (delta - param).astype(jnp.bfloat16))


def column_block(whole_rows, like, block_index):
    width = like.shape[1]
    return lax.dynamic_slice_in_dim(whole_rows, block_index * width, width, 1)


def local(
    reps,
    shards,
    tokens,
    cotangent,
    seq_len,
    in_proj,
    in_proj_first,
    in_proj_second,
    dt_proj,
    dt_proj_first,
    dt_proj_second,
    out_proj,
    out_proj_first,
    out_proj_second,
    gate_up,
    gate_up_first,
    gate_up_second,
    down_proj,
    down_proj_first,
    down_proj_second,
    norm_gains,
    gains_first,
    gains_second,
    conv_taps,
    conv_first,
    conv_second,
    ssm_params,
    ssm_first,
    ssm_second,
):
    rep_index = lax.axis_index("rep")
    shard_index = lax.axis_index("shard")
    core = lax.rem(rep_index, 2)
    lane = min(128, out_proj_first.shape[1])
    token_local = jnp.sum(seq_len).astype(jnp.float32)
    low_in = lax.all_gather(own_half(in_proj, core), "shard", axis=0, tiled=True)
    full_in = with_swapped(low_in, reps)
    small = jnp.concatenate(
        [dt_proj.reshape(-1), norm_gains.reshape(-1), conv_taps.reshape(-1)]
    ).astype(jnp.bfloat16)
    small = lax.all_gather(small, "shard", axis=0)
    dt_size, gain_size = dt_proj.size, norm_gains.size
    full_dt = small[:, :dt_size].reshape(D, MIXER_HEADS)
    full_gains = small[:, dt_size : dt_size + gain_size].reshape(-1)
    full_conv = (
        small[:, dt_size + gain_size :]
        .reshape(shards, KCONV + 1, CONV // shards)
        .transpose(1, 0, 2)
        .reshape(KCONV + 1, CONV)
    )
    width = out_proj.shape[1] // 2
    rest_parts = [
        own_half(out_proj, core),
        stack_columns(own_half(gate_up, core), width),
        own_half(down_proj, core),
    ]
    rest_cuts = (rest_parts[0].shape[0], rest_parts[0].shape[0] + rest_parts[1].shape[0])
    rest = lax.all_gather(jnp.concatenate(rest_parts, axis=0), "shard", axis=0)
    count_of_rows = tokens.shape[0]
    row_alive, token_position, pair_mask = layout(seq_len, count_of_rows)
    inputs = tokens.astype(jnp.float32)
    gains_full = full_gains.astype(jnp.float32)
    conv_full = full_conv.astype(jnp.float32)
    normed_value, norm_back = jax.vjp(rms_scale, inputs, gains_full[:D])
    normed = normed_value.astype(jnp.bfloat16)
    main_proj = forward_product(normed, full_in, core)
    dt_raw = jnp.dot(normed, full_dt, preferred_element_type=jnp.float32)
    projected_input = jnp.concatenate(
        [main_proj[:, : MIXER_WIDTH + CONV], dt_raw, main_proj[:, MIXER_WIDTH + CONV :]], axis=1
    )
    split_boundary = MIXER_WIDTH + CONV + MIXER_HEADS
    mixer_value, mixer_back = jax.vjp(
        lambda proj_part, conv_part, ssm_part, gain_part: mixer_core(
            proj_part, conv_part, ssm_part, gain_part, pair_mask, token_position
        ),
        projected_input[:, :split_boundary],
        conv_full,
        ssm_params,
        gains_full[2 * D :],
    )
    mixer_low = mixer_value.astype(jnp.bfloat16)
    rotary_output, rope_back = jax.vjp(
        lambda query_key_pair: rotary_pair(query_key_pair, token_position),
        projected_input[
            :, split_boundary : split_boundary + (QUERY_HEADS + KEY_VALUE_HEADS) * HEAD_SIZE
        ],
    )
    query_group_width = QUERY_HEADS // KEY_VALUE_HEADS
    query_rows = (
        rotary_output[:, : QUERY_HEADS * HEAD_SIZE]
        .astype(jnp.bfloat16)
        .reshape(count_of_rows, KEY_VALUE_HEADS, query_group_width, HEAD_SIZE)
    )
    key_reduced = (
        rotary_output[:, QUERY_HEADS * HEAD_SIZE :]
        .astype(jnp.bfloat16)
        .reshape(count_of_rows, KEY_VALUE_HEADS, HEAD_SIZE)
    )
    value_reduced = (
        projected_input[:, split_boundary + (QUERY_HEADS + KEY_VALUE_HEADS) * HEAD_SIZE :]
        .astype(jnp.bfloat16)
        .reshape(count_of_rows, KEY_VALUE_HEADS, HEAD_SIZE)
    )
    scores = masked_scores(query_rows, key_reduced, pair_mask)
    log_total = jax.nn.logsumexp(scores, axis=-1, keepdims=True)
    probs_low = jnp.exp(scores - log_total).astype(jnp.bfloat16)
    attended = jnp.einsum(
        "kgts,skd->tkgd", probs_low, value_reduced, preferred_element_type=jnp.float32
    )
    attended_low = attended.reshape(count_of_rows, QUERY_HEADS * HEAD_SIZE).astype(jnp.bfloat16)
    branch_in = jnp.concatenate([mixer_low, attended_low * ATT_MULT], axis=1)
    rest, branch_in = lax.optimization_barrier((rest, branch_in))
    full_out = with_swapped(unstack_gathered(rest[:, : rest_cuts[0]], out_proj.shape[0]), reps)
    full_gu = with_swapped(
        unstack_gathered(rest[:, rest_cuts[0] : rest_cuts[1]], gate_up.shape[0]), reps
    )
    full_down = with_swapped(unstack_gathered(rest[:, rest_cuts[1] :], down_proj.shape[0]), reps)
    branch = forward_product(branch_in, full_out, core)
    hidden = inputs + branch
    normed_two_value, norm_two_back = jax.vjp(rms_scale, hidden, gains_full[D : 2 * D])
    normed_two = normed_two_value.astype(jnp.bfloat16)
    gate_vals = forward_product(normed_two, full_gu, core)
    act_value, swiglu_back = jax.vjp(swiglu, gate_vals)
    act_low = act_value.astype(jnp.bfloat16)
    output = hidden + forward_product(act_low, full_down, core)
    upstream = cotangent.astype(jnp.float32) * row_alive[:, None].astype(jnp.float32)
    upstream_low = upstream.astype(jnp.bfloat16)
    grad_down = pair_gradient(act_low, upstream_low, core, reps)
    d_act = backward_product(upstream_low, full_down, core)
    (d_gate_vals,) = swiglu_back(d_act)
    d_gate_low = d_gate_vals.astype(jnp.bfloat16)
    grad_gu = pair_gradient(normed_two, d_gate_low, core, reps)
    d_normed_two = backward_product(d_gate_low, full_gu, core)
    d_hidden_norm, d_gain_two = norm_two_back(d_normed_two)
    d_hidden = upstream + d_hidden_norm
    d_branch_low = d_hidden.astype(jnp.bfloat16)
    packed = packed_blocks((grad_down, grad_gu), shards, lane)
    packed, d_branch_low = lax.optimization_barrier((packed, d_branch_low))
    owned_down, owned_gu = owned_blocks(packed, down_proj, reps)
    grad_out = pair_gradient(branch_in, d_branch_low, core, reps)
    d_branch_in = backward_product(d_branch_low, full_out, core)
    mixer_projection_gradient, d_conv, d_ssm, d_gain_mix = mixer_back(d_branch_in[:, :MIXER_WIDTH])
    d_attended = (
        (d_branch_in[:, MIXER_WIDTH:] * ATT_MULT)
        .astype(jnp.bfloat16)
        .reshape(count_of_rows, KEY_VALUE_HEADS, query_group_width, HEAD_SIZE)
    )
    probs = jnp.exp(masked_scores(query_rows, key_reduced, pair_mask) - log_total)
    d_probs = jnp.einsum(
        "tkgd,skd->kgts", d_attended, value_reduced, preferred_element_type=jnp.float32
    )
    value_gradient = jnp.einsum(
        "kgts,tkgd->skd", probs.astype(jnp.bfloat16), d_attended, preferred_element_type=jnp.float32
    )
    row_delta = jnp.sum(probs * d_probs, axis=-1, keepdims=True)
    d_scores = (probs * (d_probs - row_delta)).astype(jnp.bfloat16)
    query_gradient = jnp.einsum(
        "kgts,skd->tkgd", d_scores, key_reduced, preferred_element_type=jnp.float32
    ) * HEAD_SIZE ** (-0.5)
    key_gradient = jnp.einsum(
        "kgts,tkgd->skd", d_scores, query_rows, preferred_element_type=jnp.float32
    ) * HEAD_SIZE ** (-0.5)
    (query_key_gradient,) = rope_back(
        jnp.concatenate(
            [
                query_gradient.reshape(count_of_rows, QUERY_HEADS * HEAD_SIZE),
                key_gradient.reshape(count_of_rows, KEY_VALUE_HEADS * HEAD_SIZE),
            ],
            axis=1,
        )
    )
    d_projected = jnp.concatenate(
        [
            mixer_projection_gradient,
            query_key_gradient,
            value_gradient.reshape(count_of_rows, KEY_VALUE_HEADS * HEAD_SIZE),
        ],
        axis=1,
    ).astype(jnp.bfloat16)
    d_main = jnp.concatenate(
        [d_projected[:, : MIXER_WIDTH + CONV], d_projected[:, split_boundary:]], axis=1
    )
    d_dt = d_projected[:, MIXER_WIDTH + CONV : split_boundary]
    grad_in = pair_gradient(normed, d_main, core, reps)
    packed = packed_blocks((grad_out, grad_in), shards, lane)
    packed, d_main, d_dt = lax.optimization_barrier((packed, d_main, d_dt))
    owned_out, owned_in = owned_blocks(packed, out_proj, reps)
    grad_dt = left_product(normed, d_dt)
    d_normed = backward_product(d_main, full_in, core) + right_product(d_dt, full_dt)
    d_inputs, d_gain_one = norm_back(d_normed)
    token_grad = (d_hidden + d_inputs).astype(jnp.bfloat16)
    grad_gains = jnp.concatenate([d_gain_one, d_gain_two, d_gain_mix], axis=0)
    small_sum = total_over_mesh(
        jnp.concatenate(
            [
                grad_dt.reshape(-1),
                grad_gains,
                d_conv.reshape(-1),
                d_ssm.reshape(-1),
                token_local[None],
            ]
        ),
        reps,
        shards,
    )
    owned = (owned_down, owned_gu, owned_out, owned_in)
    owned, small_sum = lax.optimization_barrier((owned, small_sum))
    groups = [list(range(c, reps, 2)) for c in range(2)]
    summed = lax.psum_scatter(
        jnp.concatenate(owned, axis=1).reshape(-1, lane),
        "rep",
        scatter_dimension=0,
        axis_index_groups=groups,
        tiled=True,
    ).astype(jnp.float32)
    piece_cuts = [0]
    for part in owned:
        piece_cuts.append(piece_cuts[-1] + part.shape[1])
    summed_down, summed_gu, summed_out, summed_in = [
        unstack_columns(summed[piece_cuts[i] : piece_cuts[i + 1]], like.shape[0])
        for i, like in enumerate((down_proj, gate_up, out_proj, in_proj))
    ]
    cut_dt = grad_dt.size
    cut_gains = cut_dt + grad_gains.size
    cut_conv = cut_gains + d_conv.size
    summed_dt = lax.dynamic_slice_in_dim(small_sum[:cut_dt], shard_index * dt_size, dt_size, 0)
    summed_dt = summed_dt.reshape(dt_proj.shape)
    summed_gains = lax.dynamic_slice_in_dim(
        small_sum[cut_dt:cut_gains], shard_index * gain_size, gain_size, 0
    )
    summed_conv = lax.dynamic_slice_in_dim(
        small_sum[cut_gains:cut_conv].reshape(d_conv.shape),
        shard_index * conv_taps.shape[1],
        conv_taps.shape[1],
        1,
    )
    ssm_total = small_sum[cut_conv:-1].reshape(d_ssm.shape)
    token_count = small_sum[-1]
    in_piece = column_block(in_proj, in_proj_first, rep_index)
    out_piece = column_block(out_proj, out_proj_first, rep_index)
    gu_piece = column_block(gate_up, gate_up_first, rep_index)
    down_piece = column_block(down_proj, down_proj_first, rep_index)
    in_first_new, in_second_new, in_delta = adam_delta(
        in_piece, in_proj_first, in_proj_second, summed_in / token_count, 0.7 * D ** (-0.5), 0.1
    )
    out_first_new, out_second_new, out_delta = adam_delta(
        out_piece,
        out_proj_first,
        out_proj_second,
        summed_out / token_count,
        0.7 * NOUT ** (-0.5),
        0.1,
    )
    gu_first_new, gu_second_new, gu_delta = adam_delta(
        gu_piece, gate_up_first, gate_up_second, summed_gu / token_count, 0.7 * D ** (-0.5), 0.1
    )
    down_first_new, down_second_new, down_delta = adam_delta(
        down_piece,
        down_proj_first,
        down_proj_second,
        summed_down / token_count,
        0.7 * FF ** (-0.5),
        0.1,
    )
    deltas = lax.all_gather(
        jnp.concatenate(
            [stack_columns(delta, lane) for delta in (down_delta, gu_delta, out_delta, in_delta)],
            axis=0,
        ),
        "rep",
        axis=0,
    )
    whole_deltas = [
        lax.optimization_barrier(
            unstack_columns(deltas[:, piece_cuts[i] : piece_cuts[i + 1]], weight.shape[0])
        )
        for i, weight in enumerate((down_proj, gate_up, out_proj, in_proj))
    ]
    down_new, gu_new, out_new, in_new = [
        weight + delta.astype(jnp.float32)
        for weight, delta in zip((down_proj, gate_up, out_proj, in_proj), whole_deltas)
    ]
    dt_first_new, dt_second_new, dt_new = adam_update(
        dt_proj, dt_proj_first, dt_proj_second, summed_dt / token_count, 0.7 * D ** (-0.5), 0.1
    )
    gain_first_new, gain_second_new, gain_new = adam_update(
        norm_gains, gains_first, gains_second, summed_gains / token_count, 0.3, 0.0
    )
    conv_first_new, conv_second_new, conv_new = adam_update(
        conv_taps, conv_first, conv_second, summed_conv / token_count, 0.3, 0.1
    )
    ssm_first_new, ssm_second_new, ssm_new = adam_update(
        ssm_params, ssm_first, ssm_second, ssm_total / token_count, 0.8, 0.0
    )
    return (
        output.astype(jnp.bfloat16),
        token_grad,
        in_first_new,
        in_second_new,
        in_new,
        dt_first_new,
        dt_second_new,
        dt_new,
        out_first_new,
        out_second_new,
        out_new,
        gu_first_new,
        gu_second_new,
        gu_new,
        down_first_new,
        down_second_new,
        down_new,
        gain_first_new,
        gain_second_new,
        gain_new,
        conv_first_new,
        conv_second_new,
        conv_new,
        ssm_first_new,
        ssm_second_new,
        ssm_new,
    )


def solution(mesh):
    in_specs = (
        P(("rep", "shard"), None),
        P(("rep", "shard"), None),
        P(("rep", "shard")),
        P("shard", None),
        P("shard", "rep"),
        P("shard", "rep"),
        P("shard", None),
        P("shard", None),
        P("shard", None),
        P("shard", None),
        P("shard", "rep"),
        P("shard", "rep"),
        P("shard", None),
        P("shard", "rep"),
        P("shard", "rep"),
        P("shard", None),
        P("shard", "rep"),
        P("shard", "rep"),
        P("shard"),
        P("shard"),
        P("shard"),
        P(None, "shard"),
        P(None, "shard"),
        P(None, "shard"),
        P(),
        P(),
        P(),
    )
    out_specs = (
        P(("rep", "shard"), None),
        P(("rep", "shard"), None),
        P("shard", "rep"),
        P("shard", "rep"),
        P("shard", None),
        P("shard", None),
        P("shard", None),
        P("shard", None),
        P("shard", "rep"),
        P("shard", "rep"),
        P("shard", None),
        P("shard", "rep"),
        P("shard", "rep"),
        P("shard", None),
        P("shard", "rep"),
        P("shard", "rep"),
        P("shard", None),
        P("shard"),
        P("shard"),
        P("shard"),
        P(None, "shard"),
        P(None, "shard"),
        P(None, "shard"),
        P(),
        P(),
        P(),
    )
    step = functools.partial(local, mesh.shape["rep"], mesh.shape["shard"])
    return jax.shard_map(step, mesh=mesh, in_specs=in_specs, out_specs=out_specs, check_vma=False)
```
